256 devices in a mesh: section: 4 (over x_hi, core), dp: 64 (over x_lo, y, z).
Axes of the slice: x: 4 (x_hi: 2, x_lo: 2; x = x_hi * 2 + x_lo), y: 4, z: 8, core: 2. Of those that a mesh axis runs over, the one named last changes fastest.
Arguments:
- currents: bfloat16 [2, 2, 8192, 1024], P(None, None, 'dp'), may hold values from -6 to 6
- weights: bfloat16 [2, 4, 1024, 1024], P(None, 'section'), may hold values from -0.1875 to 0.1875
- decay: float32 [2, 4, 1024], P(None, 'section'), may hold values from 0.2 to 0.95
- out_grad: bfloat16 [2, 2, 8192, 1024], P(None, None, 'dp'), may hold values from -0.09375 to 0.09375
Outputs:
- grad_weights: bfloat16 [2, 4, 1024, 1024], P(None, 'section', 'dp')
- grad_decay: float32 [2, 4, 1024], P(None, 'section', 'dp')
The draws below stay inside these ranges and needn't reach their ends.
All inputs are finite; a program needn't handle non-finite values.
Results may differ from the reference program's by a relative error of at most 0.018.
The reference program's roundings to bfloat16 on the way count: a program that leaves them out, or rounds other values in their place, can miss the bound.
Values may be sent and summed in bfloat16 or wider, within the bound.
A program may use at most 128 MiB of HBM per device.

```python
import math
import jax
import jax.numpy as jnp
from jax import lax

C = 1024
ROWS = 128
MICRO = 2
STEPS = 2
ROWS_ALL = 8192
N_SECTION = 4
N_DP = 64


def with_spikes(drawn, stream_key, source, target, shards_of, factor):
    owner, partner = [(jnp.arange(drawn.shape[axis_at]) // (drawn.shape[axis_at] // shards_of)).reshape([-1 if axis == axis_at else 1 for axis in range(drawn.ndim)]) for axis_at in (source, target)]
    chosen = jax.random.permutation(stream_key, shards_of)[partner]
    strong = (owner == chosen) | (owner == (partner + shards_of // 2) % shards_of)
    return jnp.where(strong, factor * drawn, drawn)


def block_scale(key, dims, shards, least, top_value):
    def one(position, shards_of):
        heights = jax.random.uniform(jax.random.fold_in(jax.random.fold_in(key, 6), position), (shards_of,), jnp.float32, least / len(shards), top_value / len(shards))
        return jnp.repeat(jnp.exp(heights), dims[position] // shards_of).reshape((-1,) + (1,) * (len(dims) - position - 1))

    level = one(*shards[0])
    for cut in shards[1:]:
        level = level * one(*cut)
    return level


def centred(stream_key, dims, scale, limit, pieces=(), held_as=jnp.bfloat16):
    drawn = jax.random.normal(stream_key, dims, jnp.float32) * scale
    if len(pieces) > 0:
        drawn = block_scale(stream_key, dims, pieces, -0.22, 0.18) * drawn
    return jnp.clip(drawn, min=-limit, max=limit).astype(held_as)


def noise_with(stream_key, shape, scale, most, cuts, heavy, held_as=jnp.bfloat16):
    array = scale * jax.random.normal(stream_key, shape, jnp.float32)
    if cuts:
        array = array * block_scale(stream_key, shape, cuts, -0.22, 0.18)
    return jnp.clip(with_spikes(array, jax.random.fold_in(stream_key, 3), *heavy), -most, most).astype(held_as)


def setup_inputs(seed: int = 0) -> dict:
    keys = jax.random.split(jax.random.key(seed), 5)
    return {
        "currents": centred(keys[0], (MICRO, STEPS, ROWS_ALL, C), 1.0, 6.0, ((2, 64),)),
        "weights": centred(keys[1], (2, N_SECTION, C, C), C ** -0.5, 0.1875, ((1, 4),)),
        "decay": jnp.clip(jnp.exp(math.log(0.95) - 1.5581446 * jax.random.uniform(keys[2], (2, N_SECTION, C), jnp.float32) ** block_scale(keys[2], (2, N_SECTION, C), ((1, 4),), -0.2, 0.2)), 0.2, 0.95),
        "out_grad": noise_with(keys[3], (MICRO, STEPS, ROWS_ALL, C), (1.0 / (MICRO * STEPS * ROWS * N_DP) ** 0.5), 0.09375, ((2, 64),), (2, 3, 64, 4.0)),
    }


spike_gain = 4.0


def membranes(section_in, weight, decay_rate):
    result = []
    voltage = None
    for instant in range(section_in.shape[0]):
        pre = jnp.dot(section_in[instant], weight, preferred_element_type=jnp.float32)
        if instant == 0:
            level = pre
        else:
            level = decay_rate * voltage + pre
        spikes = jax.nn.sigmoid(spike_gain * (level - 1.0))
        voltage = level * (1.0 - spikes)
        result.append(level)
    return jnp.stack(result)


def backward_section(section_in, membrane, incoming, weight, decay_rate):
    spikes = jax.nn.sigmoid(spike_gain * (membrane - 1.0))
    voltage = membrane * (1.0 - spikes)
    spike_slope = spike_gain * spikes * (1.0 - spikes)
    keep_slope = (1.0 - spikes) - membrane * spike_slope
    step_count = section_in.shape[0]
    carried = jnp.zeros(membrane.shape[1:], jnp.float32)
    dweight = jnp.zeros((weight.shape[0], weight.shape[1]), jnp.float32)
    ddecay = jnp.zeros((weight.shape[1],), jnp.float32)
    results = [None] * step_count
    for instant in reversed(range(step_count)):
        grad_h = incoming[instant].astype(jnp.float32) * spike_slope[instant] + carried * keep_slope[instant]
        grad_round = grad_h.astype(jnp.bfloat16)
        dweight = dweight + lax.dot_general(section_in[instant], grad_round, (((0,), (0,)), ((), ())), preferred_element_type=jnp.float32)
        back = lax.dot_general(grad_round, weight, (((1,), (1,)), ((), ())), preferred_element_type=jnp.float32)
        results[instant] = (incoming[instant].astype(jnp.float32) + back).astype(jnp.bfloat16)
        if instant > 0:
            ddecay = ddecay + jnp.sum(grad_h * voltage[instant - 1], axis=0)
        carried = decay_rate * grad_h
    return jnp.stack(results), dweight, ddecay


def reference(currents, weights, decay, out_grad):
    micro_count, step_count, rows_all, channels = currents.shape
    activity = currents.transpose(1, 0, 2, 3).reshape(step_count, micro_count * rows_all, channels)
    stored = []
    for virtual in range(2 * N_SECTION):
        circuit, column = divmod(virtual, N_SECTION)
        stored.append(activity)
        membrane = membranes(activity, weights[circuit, column], decay[circuit, column])
        spikes = jax.nn.sigmoid(spike_gain * (membrane - 1.0))
        activity = (activity.astype(jnp.float32) + spikes).astype(jnp.bfloat16)
    gradient = out_grad.transpose(1, 0, 2, 3).reshape(step_count, micro_count * rows_all, channels)
    grad_weights = jnp.zeros((2, N_SECTION, channels, channels), jnp.float32)
    grad_decay = jnp.zeros((2, N_SECTION, channels), jnp.float32)
    for virtual in reversed(range(2 * N_SECTION)):
        circuit, column = divmod(virtual, N_SECTION)
        weight = weights[circuit, column]
        decay_rate = decay[circuit, column]
        membrane = membranes(stored[virtual], weight, decay_rate)
        gradient, dweight, ddecay = backward_section(stored[virtual], membrane, gradient, weight, decay_rate)
        grad_weights = grad_weights.at[circuit, column].set(dweight)
        grad_decay = grad_decay.at[circuit, column].set(ddecay)
    return grad_weights.astype(jnp.bfloat16), grad_decay
```

```python
import functools

import jax
import jax.numpy as jnp
from jax import lax
from jax.experimental import pallas as pl
from jax.experimental.pallas import tpu as pltpu
from jax.sharding import PartitionSpec as P

MESH = pl.DeviceIdType.MESH
F32 = jnp.float32
BF16 = jnp.bfloat16
C = 1024
ROWS = 256
HALF = 128
NY, NZ = 4, 8
GAIN = 4.0

STREAMS = (
    (0, 384, 256, ("y", "z", "x")),
    (384, 384, 128, ("z", "y", "x")),
    (768, 256, 128, ("x", "y", "z")),
)
SIZES = {"x": 2, "y": NY, "z": NZ}


def stage_plan():
    plan = {}
    for r in range(2):
        for s, (_, width, left, order) in enumerate(STREAMS):
            span = {"x": 2, "y": NY, "z": NZ}
            for axis in order:
                span[axis] = 1
                shape = (span["x"], span["y"], span["z"], 16)
                if axis == "x":
                    plan[(r, s, axis, 0, 1)] = shape + (width,)
                else:
                    for hop in range(1, SIZES[axis] // 2 + 1):
                        plan[(r, s, axis, 0, hop)] = shape + (left if hop == 1 else width,)
                        plan[(r, s, axis, 1, hop)] = shape + (width - left if hop == 1 else width,)
    return plan


PLAN = stage_plan()
KEYS = list(PLAN)


def kernel(currents, weights, decay, out_grad, gw_ref, gd_ref, *scratch):
    (w, act, kept, gq, g, p_act, p_gq, part, dec, dd, dd_in, dv, dy, dz, dx) = scratch[:15]
    (l_sem, dec_sem, cw_s, cw_r, xh_s, pc_r, gs, half_r, pa_s, pa_r, pg_s, pg_r, dd_s, dd_r, dv_s, dv_r, rs_s, rs_r) = scratch[15:33]
    landing = dict(zip(KEYS, scratch[33:]))
    number = {key: i for i, key in enumerate(KEYS)}

    sec = lax.axis_index("section")
    dp = lax.axis_index("dp")
    xh, c = sec // 2, sec % 2
    xl, y, z = dp // 32, (dp // 8) % 4, dp % 8

    def device(xh=xh, c=c, xl=xl, y=y, z=z):
        return (xh * 2 + c, xl * 32 + y * 8 + z)

    core = device(c=1 - c)
    to_xl = device(xl=1 - xl)
    y_by = lambda k: device(y=(y + k) % NY)
    z_by = lambda k: device(z=(z + k) % NZ)
    across = lambda core_there: device(xh=1 - xh, xl=1 - xl, c=core_there)

    def remote(src, dst, send, recv, to):
        return pltpu.make_async_remote_copy(
            src_ref=src, dst_ref=dst, send_sem=send, recv_sem=recv, device_id=to, device_id_type=MESH
        )

    local = []
    for r in range(2):
        local.append(pltpu.make_async_copy(weights.at[r], w.at[r * 4 + sec], l_sem.at[r]))
    local.append(pltpu.make_async_copy(currents.at[c], act.at[0], l_sem.at[2]))
    local.append(pltpu.make_async_copy(out_grad.at[c], g, l_sem.at[3]))
    local.append(pltpu.make_async_copy(decay, dec.at[sec], l_sem.at[4]))
    for copy in local:
        copy.start()

    partners = [core, to_xl, across(c), across(1 - c)]
    partners += [y_by(k) for k in range(1, NY)] + [z_by(k) for k in range(1, NZ)]
    barrier = pltpu.get_barrier_semaphore()
    for partner in partners:
        pl.semaphore_signal(barrier, inc=1, device_id=partner, device_id_type=MESH)
    pl.semaphore_wait(barrier, len(partners))

    colour_there = (4 * (1 - xl) + 2 * y + z) % 8
    colour = (4 * xl + 2 * y + z) % 8

    def rows_of(half, unit, low, count):
        start = half * 512 + (unit % 8) * 64 + low
        return pl.ds(pl.multiple_of(start, 32), count)

    dec_copies = []
    for i, to in enumerate((core, across(c), across(1 - c))):
        dec_copies.append(remote(decay, dec.at[sec], dec_sem.at[0, i], dec_sem.at[1, i], to))
    for copy in dec_copies:
        copy.start()
    for r in range(2):
        layer = r * 4 + sec
        for half in range(2):
            for piece, (unit, low, count) in enumerate(((0, 0, 64), (3, 0, 32))):
                rows = rows_of(half, colour_there + unit, low, count)
                remote(
                    weights.at[r, rows], w.at[layer, rows], xh_s, pc_r.at[r * 2 + c, piece], across(half)
                ).start()
        remote(weights.at[r], w.at[layer], cw_s.at[r], cw_r.at[r], core).start()

    def layer_of(q):
        return (q // 2) * 4 + (1 - xh) * 2 + q % 2

    UNITS = ((0, 0, 64), (3, 0, 32), (1, 0, 64), (7, 0, 64), (2, 0, 64), (6, 0, 64), (4, 0, 64), (3, 32, 32), (5, 0, 32), (5, 32, 32))

    def pass_on(q, unit, low, count, piece, to):
        rows = rows_of(c, colour + unit, low, count)
        here = w.at[layer_of(q), rows]
        recv = half_r.at[q] if piece is None else pc_r.at[q, piece]
        remote(here, here, gs.at[q], recv, to).start()

    def arrived(q, piece):
        unit, low, count = UNITS[piece]
        here = w.at[layer_of(q), rows_of(c, colour + unit, low, count)]
        pltpu.make_async_copy(here, here, pc_r.at[q, piece]).wait()
        pass_on(q, unit, low, count, None, core)

    def first_hop(q):
        arrived(q, 0)
        for piece, to in ((3, z_by(1)), (2, z_by(7)), (5, y_by(1)), (4, y_by(3)), (6, to_xl)):
            pass_on(q, 0, 0, 64, piece, to)

    def second_hop(q):
        arrived(q, 2)
        pass_on(q, 1, 32, 32, 7, y_by(3))
        pass_on(q, 1, 32, 32, 9, to_xl)
        arrived(q, 3)
        pass_on(q, 7, 0, 32, 8, y_by(1))

    def rest(q):
        for piece in (1, 4, 5, 6, 7, 8, 9):
            arrived(q, piece)

    def tile(j, size=256):
        return pl.ds(pl.multiple_of(j * size, size), size)

    def own_chip(layer):
        return (layer // 2) % 2 == xh

    def forward(layer):
        lap = layer // 4

        @pl.when(own_chip(layer) & (layer % 2 == c))
        def _():
            pltpu.make_async_copy(weights.at[lap], w.at[layer], l_sem.at[lap]).wait()

        @pl.when(own_chip(layer) & (layer % 2 != c))
        def _():
            pltpu.make_async_copy(w.at[layer], w.at[layer], cw_r.at[lap]).wait()
            remote(act.at[layer], p_act.at[lap], pa_s.at[lap], pa_r.at[lap], core).start()

        @pl.when(jnp.logical_not(own_chip(layer)))
        def _():
            half = w.at[layer, pl.ds(pl.multiple_of((1 - c) * 512, 512), 512)]
            pltpu.make_async_copy(half, half, half_r.at[lap * 2 + layer % 2]).wait()

        @pl.loop(0, 4)
        def _(j):
            cols = tile(j)
            pre = jnp.dot(act[layer], w[layer, :, cols], preferred_element_type=F32)
            rate = dec[layer % 4, lap, :, cols]
            old = act[layer, :, cols].astype(F32)
            h0 = pre[:HALF]
            s0 = 1.0 / (1.0 + jnp.exp(-GAIN * (h0 - 1.0)))
            rest0 = 1.0 - s0
            v0 = h0 * rest0
            h1 = rate * v0 + pre[HALF:]
            s1 = 1.0 / (1.0 + jnp.exp(-GAIN * (h1 - 1.0)))
            slope0 = GAIN * s0 * rest0
            kept[layer, 0, :, cols] = slope0
            kept[layer, 1, :, cols] = GAIN * s1 * (1.0 - s1)
            kept[layer, 2, :, cols] = rate * (rest0 - h0 * slope0)
            kept[layer, 3, :, cols] = v0
            act[layer + 1, pl.ds(0, HALF), cols] = (old[:HALF] + s0).astype(BF16)
            act[layer + 1, pl.ds(HALF, HALF), cols] = (old[HALF:] + s1).astype(BF16)

    def backward(layer, with_input=True):
        lap = layer // 4

        @pl.loop(0, 4)
        def _(j):
            cols = tile(j)
            gh1 = g[pl.ds(HALF, HALF), cols].astype(F32) * kept[layer, 1, :, cols]
            gh0 = g[pl.ds(0, HALF), cols].astype(F32) * kept[layer, 0, :, cols] + gh1 * kept[layer, 2, :, cols]
            gq[layer, pl.ds(0, HALF), cols] = gh0.astype(BF16)
            gq[layer, pl.ds(HALF, HALF), cols] = gh1.astype(BF16)
            dd[layer, :, cols] = jnp.sum(gh1 * kept[layer, 3, :, cols], axis=0, keepdims=True)

        @pl.when(own_chip(layer) & (layer % 2 != c))
        def _():
            remote(gq.at[layer], p_gq.at[lap], pg_s.at[lap], pg_r.at[lap], core).start()
            remote(dd.at[layer], dd_in.at[lap], dd_s.at[lap], dd_r.at[lap], core).start()

        if with_input:

            @pl.loop(0, 4)
            def _(j):
                cols = tile(j)
                back = lax.dot_general(
                    gq[layer], w[layer, cols, :], (((1,), (1,)), ((), ())), preferred_element_type=F32
                )
                g[:, cols] = (g[:, cols].astype(F32) + back).astype(BF16)

    def weight_gradient(lap):
        layer = lap * 4 + sec
        pltpu.make_async_copy(p_act.at[lap], p_act.at[lap], pa_r.at[lap]).wait()
        pltpu.make_async_copy(p_gq.at[lap], p_gq.at[lap], pg_r.at[lap]).wait()
        pltpu.make_async_copy(dd_in.at[lap], dd_in.at[lap], dd_r.at[lap]).wait()
        dv[pl.ds(lap, 1), :] = dd[layer] + dd_in[lap]
        over_rows = (((0,), (0,)), ((), ()))

        @pl.loop(0, 4)
        def _(i):
            for n in range(2):
                cols = pl.ds(n * 512, 512)
                total = lax.dot_general(
                    act[layer, :, tile(i)], gq[layer, :, cols], over_rows, preferred_element_type=F32
                ) + lax.dot_general(
                    p_act[lap, :, tile(i)], p_gq[lap, :, cols], over_rows, preferred_element_type=F32
                )
                part[lap, i // 2, pl.ds((i % 2) * 2, 2), :, :, cols] = total.astype(BF16).reshape(2, 8, 16, 512)

    sums = []

    def stream(r, s):
        first, width, left, order = STREAMS[s]
        where = {"x": pl.ds(0, 2), "y": pl.ds(0, NY), "z": pl.ds(0, NZ)}
        mine = {"x": xl, "y": y, "z": z}

        def chunk(axis, place, low=0, count=width):
            at = dict(where)
            at[axis] = pl.ds(place, 1)
            return part.at[r, at["x"], at["y"], at["z"], :, pl.ds(first + low, count)]

        def send(src, key, to):
            i = number[key]
            copy = remote(src, landing[key], rs_s.at[i], rs_r.at[i], to)
            copy.start()
            sums.append(copy)

        def wait(key):
            i = number[key]
            pltpu.make_async_copy(landing[key], landing[key], rs_r.at[i]).wait()

        for axis in order:
            last = axis == order[-1]
            n = SIZES[axis]
            me = mine[axis]
            if axis == "x":
                key = (r, s, axis, 0, 1)
                send(chunk(axis, 1 - me), key, to_xl)
                yield
                wait(key)
                terms = [landing[key][...]]
            else:
                by = y_by if axis == "y" else z_by
                far = n // 2
                send(chunk(axis, (me + far) % n, 0, left), (r, s, axis, 0, 1), by(1))
                send(chunk(axis, (me + far) % n, left, width - left), (r, s, axis, 1, 1), by(n - 1))
                yield
                for hop in range(2, far + 1):
                    for way in range(2):
                        step = far - hop + 1
                        place = (me + (step if way == 0 else n - step)) % n
                        came = (r, s, axis, way, hop - 1)
                        wait(came)
                        low, count = (0, width) if hop > 2 else ((0, left) if way == 0 else (left, width - left))
                        here = chunk(axis, place, low, count)
                        here[...] = (here[...].astype(F32) + landing[came][...].astype(F32)).astype(BF16)
                        send(chunk(axis, place), (r, s, axis, way, hop), by(1 if way == 0 else n - 1))
                    yield
                for way in range(2):
                    wait((r, s, axis, way, far))
                terms = [landing[(r, s, axis, way, far)][...] for way in range(2)]
            own = chunk(axis, me)
            total = own[...].astype(F32)
            for term in terms:
                total = total + term.astype(F32)
            where[axis] = pl.ds(me, 1)
            if last:
                gw_ref[r, :, pl.ds(first, width)] = total.astype(BF16).reshape(16, width)
            else:
                own[...] = total.astype(BF16)

    def advance(streams):
        going = []
        for one in streams:
            try:
                next(one)
                going.append(one)
            except StopIteration:
                pass
        return going

    start = 2 - 2 * xh
    local[2].wait()
    local[4].wait()
    for copy in dec_copies:
        copy.wait_recv()

    def forward_loop(low, high):
        def body(layer, carry):
            forward(layer)
            return carry

        lax.fori_loop(low, high, body, 0)

    forward_loop(0, start)
    for q in (0, 1):
        first_hop(q)
    for q in (0, 1):
        second_hop(q)
    for q in (0, 1):
        rest(q)
    forward(start)
    first_hop(2)
    forward(start + 1)
    first_hop(3)
    second_hop(2)
    forward(start + 2)
    second_hop(3)
    forward(start + 3)
    rest(2)
    rest(3)
    forward_loop(start + 4, 8)

    local[3].wait()
    count = 4 - 2 * xh

    def body(i, carry):
        backward(7 - i)
        return carry

    lax.fori_loop(0, count, body, 0)
    weight_gradient(1)
    streams = advance([stream(1, s) for s in range(len(STREAMS))])
    for i in range(4):
        backward(7 - count - i, with_input=i < 3)
        streams = advance(streams)
    weight_gradient(0)
    streams = streams + [stream(0, s) for s in range(len(STREAMS))]
    streams = advance(streams[-len(STREAMS):]) + streams[: -len(STREAMS)]

    decay_copies = []

    def swap(buffer, by, n, base):
        copies = []
        for k in range(1, n):
            copies.append(remote(dv, buffer.at[k - 1], dv_s.at[base + k], dv_r.at[base + k], by(k)))
            copies[-1].start()
        return copies

    def gather_in(copies, buffer):
        for copy in copies:
            copy.wait()
        total = dv[...]
        for k in range(len(copies)):
            total = total + buffer[k]
        dv[...] = total

    copies = swap(dy, y_by, NY, 0)
    streams = advance(streams)
    gather_in(copies, dy)
    copies = swap(dz, z_by, NZ, 8)
    streams = advance(streams)
    streams = advance(streams)
    gather_in(copies, dz)
    copies = swap(dx, lambda k: to_xl, 2, 20)
    streams = advance(streams)
    gather_in(copies, dx)
    gd_ref[...] = pltpu.roll(dv[...], (C - dp * 16) % C, axis=1)[:, :16]
    while streams:
        streams = advance(streams)

    for copy in sums:
        copy.wait_send()
    for copy in dec_copies:
        copy.wait_send()
    sent = w.at[0, pl.ds(0, 384)]
    pltpu.make_async_copy(sent, sent, xh_s).wait()
    for q in range(4):
        sent = w.at[0, pl.ds(0, 928)]
        pltpu.make_async_copy(sent, sent, gs.at[q]).wait()
    for r in range(2):
        pltpu.make_async_copy(w.at[0], w.at[0], cw_s.at[r]).wait()
        pltpu.make_async_copy(p_act.at[r], p_act.at[r], pa_s.at[r]).wait()
        pltpu.make_async_copy(p_gq.at[r], p_gq.at[r], pg_s.at[r]).wait()
        pltpu.make_async_copy(dd_in.at[r], dd_in.at[r], dd_s.at[r]).wait()


def on_device(currents, weights, decay, out_grad):
    dma = pltpu.SemaphoreType.DMA
    vmem = pltpu.VMEM
    scratch = [
        vmem((8, C, C), BF16),
        vmem((9, ROWS, C), BF16),
        vmem((8, 4, HALF, C), F32),
        vmem((8, ROWS, C), BF16),
        vmem((ROWS, C), BF16),
        vmem((2, ROWS, C), BF16),
        vmem((2, ROWS, C), BF16),
        vmem((2, 2, NY, NZ, 16, C), BF16),
        vmem((4, 2, 1, C), F32),
        vmem((8, 1, C), F32),
        vmem((2, 1, C), F32),
        vmem((2, C), F32),
        vmem((NY - 1, 2, C), F32),
        vmem((NZ - 1, 2, C), F32),
        vmem((1, 2, C), F32),
        dma((5,)), dma((2, 3)), dma((2,)), dma((2,)), dma, dma((4, 10)), dma((4,)), dma((4,)),
        dma((2,)), dma((2,)), dma((2,)), dma((2,)), dma((2,)), dma((2,)), dma((24,)), dma((24,)),
        dma((len(KEYS),)), dma((len(KEYS),)),
    ] + [vmem(PLAN[key], BF16) for key in KEYS]
    anywhere = pl.BlockSpec(memory_space=pl.ANY)
    in_vmem = pl.BlockSpec(memory_space=pltpu.VMEM)
    gw, gd = pl.pallas_call(
        kernel,
        out_shape=(jax.ShapeDtypeStruct((2, 16, C), BF16), jax.ShapeDtypeStruct((2, 16), F32)),
        in_specs=[anywhere] * 4,
        out_specs=(in_vmem, in_vmem),
        scratch_shapes=scratch,
        compiler_params=pltpu.CompilerParams(
            collective_id=0, has_side_effects=True, vmem_limit_bytes=60 * 2**20
        ),
        name="relay",
    )(
        currents.reshape(2, ROWS, C),
        weights.reshape(2, C, C),
        decay,
        out_grad.reshape(2, ROWS, C),
    )
    return gw[:, None], gd[:, None]


def solution(mesh):
    in_specs = (
        P(None, None, "dp", None),
        P(None, "section", None, None),
        P(None, "section", None),
        P(None, None, "dp", None),
    )
    out_specs = (P(None, "section", "dp", None), P(None, "section", "dp"))
    return jax.shard_map(on_device, mesh=mesh, in_specs=in_specs, out_specs=out_specs, check_vma=False)
```

```python
import functools
import itertools

import jax
import jax.numpy as jnp
from jax import lax
from jax.experimental import pallas as pl
from jax.experimental.pallas import tpu as pltpu
from jax.sharding import PartitionSpec as P

MESH = pl.DeviceIdType.MESH
F32 = jnp.float32
BF16 = jnp.bfloat16
C = 1024
ROWS = 256
HALF = 128
NY, NZ = 4, 8
GAIN = 4.0

SUBS = 2
WINDOW = 1
UNIT = 64 // SUBS
X, Y, Z, ZD, YD, XYD = "x", "y", "z", "zd", "yd", "xyd"

STREAMS = (
    (
        (0, 2, (Z, Y, X,), -1),
        (2, 2, (X, Y, ZD,), -1),
        (4, 2, (Z, XYD,), -1),
        (6, 1, (Y, Z, X,), 1),
        (7, 1, (X, Y, ZD,), -1),
    ),
    (
        (0, 2, (X, Y, Z,), 1),
        (2, 2, (Z, YD, X,), 1),
        (4, 2, (Y, Z, X,), -1),
        (6, 2, (Y, Z, X,), 1),
    ),
)
ORDER = (
    16, 17, -1, 18, 19, -1, -1, -1, 17, 17, -1, -1, -2, 0, 18, 1, -1, 3, 2, 17,
    16, 19, 0, 0, 4, 17, 3, -2, 2, 2, 18, 16, 0, 17, 0, 1, 19, 2, 18, 18,
    3, 2, 4, -2, 0, 16, 1, 19, 19, 17, 3, 3, 18, 18, 2, 4, 16, 19, 0, 3,
    16, 3, 19, 18, 1, 16, 19, 3, 0, -2, 16, 2, 4, 16, 0, 17, 3, 18, 19, 1,
    0, 16, 2, 3, 17, 18, 19, 4,
)
SIZES = {"x": 2, "y": NY, "z": NZ}


def offsets(stage):
    return [o for o in itertools.product(*[range(SIZES[axis]) for axis in stage.rstrip("d")]) if any(o)]


def hops_of(axis, way):
    far = SIZES[axis] // 2
    return {way: far, -way: far - 1}


def landing_plan():
    plan = {}
    for r in range(2):
        for s, (_, blocks, order, way) in enumerate(STREAMS[r]):
            span = dict(SIZES)
            for stage in order:
                for axis in stage.rstrip("d"):
                    span[axis] = 1
                shape = (blocks, span["x"], span["y"], span["z"], 16, 128)
                if stage in ("y", "z"):
                    for d, count in hops_of(stage, way).items():
                        for hop in range(1, count + 1):
                            plan[(r, s, stage, d, hop)] = shape
                else:
                    for offset in offsets(stage):
                        plan[(r, s, stage, offset)] = shape
    return plan


PLAN = landing_plan()
KEYS = list(PLAN)


def kernel(currents, weights, decay, out_grad, gw_ref, gd_ref, *scratch):
    (w, act, kept, gq, g, p_act, p_gq, part, dec, dd, dd_in, dv, dy, dz, dx) = scratch[:15]
    (l_sem, dec_sem, cw_s, cw_r, xh_s, pc_r, gs, half_r, pa_s, pa_r, pg_s, pg_r, dd_s, dd_r, dv_s, dv_r, rs_s, rs_r) = scratch[15:33]
    landing = dict(zip(KEYS, scratch[33:]))
    number = {key: i for i, key in enumerate(KEYS)}

    sec = lax.axis_index("section")
    dp = lax.axis_index("dp")
    xh, c = sec // 2, sec % 2
    xl, y, z = dp // 32, (dp // 8) % 4, dp % 8

    def device(xh=xh, c=c, xl=xl, y=y, z=z):
        return (xh * 2 + c, xl * 32 + y * 8 + z)

    core = device(c=1 - c)
    to_xl = device(xl=1 - xl)
    y_by = lambda k: device(y=(y + k) % NY)
    z_by = lambda k: device(z=(z + k) % NZ)
    across = lambda core_there: device(xh=1 - xh, xl=1 - xl, c=core_there)

    def remote(src, dst, send, recv, to):
        return pltpu.make_async_remote_copy(
            src_ref=src, dst_ref=dst, send_sem=send, recv_sem=recv, device_id=to, device_id_type=MESH
        )

    local = []
    for r in range(2):
        local.append(pltpu.make_async_copy(weights.at[r], w.at[r * 4 + sec], l_sem.at[r]))
    local.append(pltpu.make_async_copy(currents.at[c], act.at[0], l_sem.at[2]))
    local.append(pltpu.make_async_copy(out_grad.at[c], g, l_sem.at[3]))
    local.append(pltpu.make_async_copy(decay, dec.at[sec], l_sem.at[4]))
    for copy in local:
        copy.start()

    partners = [core, to_xl, across(c), across(1 - c)]
    partners += [y_by(k) for k in range(1, NY)] + [z_by(k) for k in range(1, NZ)]
    partners += [device(xl=1 - xl, y=(y + k) % NY) for k in range(1, NY)]
    barrier = pltpu.get_barrier_semaphore()
    for partner in partners:
        pl.semaphore_signal(barrier, inc=1, device_id=partner, device_id_type=MESH)
    pl.semaphore_wait(barrier, len(partners))

    colour_there = (4 * (1 - xl) + 2 * y + z) % 8
    colour = (4 * xl + 2 * y + z) % 8

    def rows_of(half, sub, unit, low, count):
        start = half * 512 + sub * (512 // SUBS) + (unit % 8) * UNIT + low
        return pl.ds(pl.multiple_of(start, 16), count)

    dec_copies = []
    for i, to in enumerate((core, across(c), across(1 - c))):
        dec_copies.append(remote(decay, dec.at[sec], dec_sem.at[0, i], dec_sem.at[1, i], to))
    for copy in dec_copies:
        copy.start()

    def send_across(phase):
        r, sub = divmod(phase, SUBS)
        for piece, (unit, count) in enumerate(((0, UNIT), (3, UNIT // 2))):
            for half in range(2):
                rows = rows_of(half, sub, colour_there + unit, 0, count)
                remote(
                    weights.at[r, rows], w.at[r * 4 + sec, rows], xh_s, pc_r.at[r * 2 + c, sub, piece], across(half)
                ).start()

    for phase in range(WINDOW):
        send_across(phase)
    remote(weights.at[0], w.at[sec], cw_s.at[0], cw_r.at[0], core).start()

    def layer_of(q):
        return (q // 2) * 4 + (1 - xh) * 2 + q % 2

    low_half, high_half = (0, UNIT // 2), (UNIT // 2, UNIT // 2)
    every = (0, UNIT)
    PIECES = (
        (0, *every), (3, *low_half), (1, *every), (7, *every), (2, *every), (6, *every), (4, *every),
        (3, *high_half), (5, *low_half), (5, *high_half),
    )

    def pass_on(q, sub, unit, low, count, piece, to):
        here = w.at[layer_of(q), rows_of(c, sub, colour + unit, low, count)]
        remote(here, here, gs.at[q], pc_r.at[q, sub, piece], to).start()

    def arrived(q, sub, piece):
        unit, low, count = PIECES[piece]
        here = w.at[layer_of(q), rows_of(c, sub, colour + unit, low, count)]
        pltpu.make_async_copy(here, here, pc_r.at[q, sub, piece]).wait()

    def both(phase):
        lap, sub = divmod(phase, SUBS)
        return ((lap * 2, sub), (lap * 2 + 1, sub))

    def first_hop(phase):
        for q, sub in both(phase):
            arrived(q, sub, 0)
            for piece, to in ((4, y_by(3)), (5, y_by(1)), (6, to_xl), (3, z_by(1)), (2, z_by(7))):
                pass_on(q, sub, 0, *every, piece, to)
        if phase + WINDOW < 2 * SUBS:
            send_across(phase + WINDOW)
        if phase == SUBS - 1:
            remote(weights.at[1], w.at[4 + sec], cw_s.at[1], cw_r.at[1], core).start()

    def second_hop(phase):
        for q, sub in both(phase):
            arrived(q, sub, 2)
            pass_on(q, sub, 1, *high_half, 7, y_by(3))
            pass_on(q, sub, 1, *high_half, 9, to_xl)
            arrived(q, sub, 3)
            pass_on(q, sub, 7, *low_half, 8, y_by(1))

    def rest(phase):
        for q, sub in both(phase):
            for piece in (1, 4, 5, 6, 7, 8, 9):
                arrived(q, sub, piece)
            start = c * 512 + sub * (512 // SUBS)
            here = w.at[layer_of(q), pl.ds(pl.multiple_of(start, 128), 512 // SUBS)]
            remote(here, here, gs.at[q], half_r.at[q, sub], core).start()

    def tile(j, size=256):
        return pl.ds(pl.multiple_of(j * size, size), size)

    def own_chip(layer):
        return (layer // 2) % 2 == xh

    def forward(layer):
        lap = layer // 4

        @pl.when(own_chip(layer) & (layer % 2 == c))
        def _():
            pltpu.make_async_copy(weights.at[lap], w.at[layer], l_sem.at[lap]).wait()

        @pl.when(own_chip(layer) & (layer % 2 != c))
        def _():
            pltpu.make_async_copy(w.at[layer], w.at[layer], cw_r.at[lap]).wait()
            remote(act.at[layer], p_act.at[lap], pa_s.at[lap], pa_r.at[lap], core).start()

        @pl.when(jnp.logical_not(own_chip(layer)))
        def _():
            for sub in range(SUBS):
                start = (1 - c) * 512 + sub * (512 // SUBS)
                here = w.at[layer, pl.ds(pl.multiple_of(start, 128), 512 // SUBS)]
                pltpu.make_async_copy(here, here, half_r.at[lap * 2 + layer % 2, sub]).wait()

        @pl.loop(0, 4, unroll=True)
        def _(j):
            cols = tile(j)
            pre = jnp.dot(act[layer], w[layer, :, cols], preferred_element_type=F32)
            rate = dec[layer % 4, lap, :, cols]
            old = act[layer, :, cols].astype(F32)
            h0 = pre[:HALF]
            s0 = 1.0 / (1.0 + jnp.exp(-GAIN * (h0 - 1.0)))
            rest0 = 1.0 - s0
            v0 = h0 * rest0
            h1 = rate * v0 + pre[HALF:]
            s1 = 1.0 / (1.0 + jnp.exp(-GAIN * (h1 - 1.0)))
            slope0 = GAIN * s0 * rest0
            kept[layer, 0, :, cols] = slope0
            kept[layer, 1, :, cols] = GAIN * s1 * (1.0 - s1)
            kept[layer, 2, :, cols] = rate * (rest0 - h0 * slope0)
            kept[layer, 3, :, cols] = v0
            act[layer + 1, pl.ds(0, HALF), cols] = (old[:HALF] + s0).astype(BF16)
            act[layer + 1, pl.ds(HALF, HALF), cols] = (old[HALF:] + s1).astype(BF16)

    def backward(layer, with_input=True):
        lap = layer // 4

        @pl.loop(0, 4, unroll=True)
        def _(j):
            cols = tile(j)
            gh1 = g[pl.ds(HALF, HALF), cols].astype(F32) * kept[layer, 1, :, cols]
            gh0 = g[pl.ds(0, HALF), cols].astype(F32) * kept[layer, 0, :, cols] + gh1 * kept[layer, 2, :, cols]
            gq[layer, pl.ds(0, HALF), cols] = gh0.astype(BF16)
            gq[layer, pl.ds(HALF, HALF), cols] = gh1.astype(BF16)
            dd[layer, :, cols] = jnp.sum(gh1 * kept[layer, 3, :, cols], axis=0, keepdims=True)

        @pl.when(own_chip(layer) & (layer % 2 != c))
        def _():
            remote(gq.at[layer], p_gq.at[lap], pg_s.at[lap], pg_r.at[lap], core).start()
            remote(dd.at[layer], dd_in.at[lap], dd_s.at[lap], dd_r.at[lap], core).start()

        if with_input:

            @pl.loop(0, 4, unroll=True)
            def _(j):
                cols = tile(j)
                back = lax.dot_general(
                    gq[layer], w[layer, cols, :], (((1,), (1,)), ((), ())), preferred_element_type=F32
                )
                g[:, cols] = (g[:, cols].astype(F32) + back).astype(BF16)

    def weight_gradient(lap, n):
        layer = lap * 4 + sec
        if n == 0:
            pltpu.make_async_copy(p_act.at[lap], p_act.at[lap], pa_r.at[lap]).wait()
            pltpu.make_async_copy(p_gq.at[lap], p_gq.at[lap], pg_r.at[lap]).wait()
            pltpu.make_async_copy(dd_in.at[lap], dd_in.at[lap], dd_r.at[lap]).wait()
            dv[pl.ds(lap, 1), :] = dd[layer] + dd_in[lap]
        over_rows = (((0,), (0,)), ((), ()))
        cols = pl.ds(n * 512, 512)

        @pl.loop(0, 4, unroll=True)
        def _(i):
            total = lax.dot_general(
                act[layer, :, tile(i)], gq[layer, :, cols], over_rows, preferred_element_type=F32
            ) + lax.dot_general(
                p_act[lap, :, tile(i)], p_gq[lap, :, cols], over_rows, preferred_element_type=F32
            )
            for b in range(4):
                block = total[:, b * 128 : (b + 1) * 128].astype(BF16).reshape(2, 8, 16, 128)
                part[lap, n * 4 + b, i // 2, pl.ds((i % 2) * 2, 2)] = block

    sums = []

    def stream(r, s):
        first, blocks, order, way = STREAMS[r][s]
        where = {"x": pl.ds(0, 2), "y": pl.ds(0, NY), "z": pl.ds(0, NZ)}
        mine = {"x": xl, "y": y, "z": z}

        def chunk(places):
            at = {**where, **{axis: pl.ds(place, 1) for axis, place in places.items()}}
            return part.at[r, pl.ds(first, blocks), at["x"], at["y"], at["z"]]

        def send(places, key, to):
            i = number[key]
            copy = remote(chunk(places), landing[key], rs_s.at[i], rs_r.at[i], to)
            copy.start()
            sums.append(copy)

        def wait(key):
            i = number[key]
            pltpu.make_async_copy(landing[key], landing[key], rs_r.at[i]).wait()

        def own_sum(keys):
            for key in keys:
                wait(key)
            total = chunk({})[...].astype(F32)
            for key in keys:
                total = total + landing[key][...].astype(F32)
            return total

        pending = []
        for stage in order:
            if pending:
                chunk({})[...] = own_sum(pending).astype(BF16)
            if stage in ("y", "z"):
                n, me = SIZES[stage], mine[stage]
                by = y_by if stage == "y" else z_by
                hops = hops_of(stage, way)
                for d in (1, -1):
                    send({stage: (me + d * hops[d] + n) % n}, (r, s, stage, d, 1), by((d + n) % n))
                yield
                for hop in range(2, n // 2 + 1):
                    for d in (way, -way):
                        if hop > hops[d]:
                            continue
                        to = {stage: (me + d * (hops[d] - hop + 1) + n) % n}
                        came = (r, s, stage, d, hop - 1)
                        wait(came)
                        here = chunk(to)
                        here[...] = (here[...].astype(F32) + landing[came][...].astype(F32)).astype(BF16)
                        send(to, (r, s, stage, d, hop), by((d + n) % n))
                        yield
                pending = [(r, s, stage, d, hops[d]) for d in (1, -1)]
                where[stage] = pl.ds(me, 1)
            else:
                axes = stage.rstrip("d")
                pending = []
                for offset in offsets(stage):
                    to = {axis: (mine[axis] + by) % SIZES[axis] for axis, by in zip(axes, offset)}
                    names = {"x": "xl", "y": "y", "z": "z"}
                    send(to, (r, s, stage, offset), device(**{names[axis]: place for axis, place in to.items()}))
                    pending.append((r, s, stage, offset))
                yield
                for axis in axes:
                    where[axis] = pl.ds(mine[axis], 1)
        total = own_sum(pending).astype(BF16)
        for b in range(blocks):
            gw_ref[r, :, pl.ds((first + b) * 128, 128)] = total[b, 0, 0, 0]

    def decay_sum():
        for i, (buffer, by, n) in enumerate(((dy, y_by, NY), (dz, z_by, NZ), (dx, lambda k: to_xl, 2))):
            copies = []
            for k in range(1, n):
                copies.append(remote(dv, buffer.at[k - 1], dv_s.at[i * 8 + k], dv_r.at[i * 8 + k], by(k)))
                copies[-1].start()
            yield
            for copy in copies:
                copy.wait()
            total = dv[...]
            for k in range(n - 1):
                total = total + buffer[k]
            dv[...] = total
        gd_ref[...] = pltpu.roll(dv[...], (C - dp * 16) % C, axis=1)[:, :16]

    start = 2 - 2 * xh
    local[2].wait()
    local[4].wait()
    for copy in dec_copies:
        copy.wait_recv()

    def forward_loop(low, high):
        def body(layer, carry):
            forward(layer)
            return carry

        lax.fori_loop(low, high, body, 0)

    forward_loop(0, start)
    done = 0
    for step in range(2 * SUBS + 2):
        if step < 2 * SUBS:
            first_hop(step)
        if 0 <= step - 1 < 2 * SUBS:
            second_hop(step - 1)
        if step - 2 >= 0:
            rest(step - 2)
        if SUBS + 1 <= step < 2 * SUBS + 1 and done < 4:
            forward(start + done)
            done += 1
    forward_loop(start + done, 8)

    local[3].wait()
    count = 4 - 2 * xh

    def body(i, carry):
        backward(7 - i)
        return carry

    lax.fori_loop(0, count, body, 0)
    weight_gradient(1, 0)
    pieces = [functools.partial(weight_gradient, 1, 1)]
    pieces += [functools.partial(backward, 7 - count - i, i < 3) for i in range(4)]
    pieces += [functools.partial(weight_gradient, 0, n) for n in range(2)]
    streams = {r * 16 + s: stream(r, s) for r in range(2) for s in range(len(STREAMS[r]))}
    streams[-2] = decay_sum()

    def advance(key):
        if key == -1:
            pieces.pop(0)()
        elif next(streams[key], 0) is not None:
            del streams[key]

    for key in ORDER:
        advance(key)
    assert not streams and not pieces

    for copy in sums:
        copy.wait_send()
    for copy in dec_copies:
        copy.wait_send()
    sent = w.at[0, pl.ds(0, 384)]
    pltpu.make_async_copy(sent, sent, xh_s).wait()
    for q in range(4):
        sent = w.at[0, pl.ds(0, 928)]
        pltpu.make_async_copy(sent, sent, gs.at[q]).wait()
    for r in range(2):
        pltpu.make_async_copy(w.at[0], w.at[0], cw_s.at[r]).wait()
        pltpu.make_async_copy(p_act.at[r], p_act.at[r], pa_s.at[r]).wait()
        pltpu.make_async_copy(p_gq.at[r], p_gq.at[r], pg_s.at[r]).wait()
        pltpu.make_async_copy(dd_in.at[r], dd_in.at[r], dd_s.at[r]).wait()


def on_device(currents, weights, decay, out_grad):
    dma = pltpu.SemaphoreType.DMA
    vmem = pltpu.VMEM
    scratch = [
        vmem((8, C, C), BF16),
        vmem((9, ROWS, C), BF16),
        vmem((8, 4, HALF, C), F32),
        vmem((8, ROWS, C), BF16),
        vmem((ROWS, C), BF16),
        vmem((2, ROWS, C), BF16),
        vmem((2, ROWS, C), BF16),
        vmem((2, 8, 2, NY, NZ, 16, 128), BF16),
        vmem((4, 2, 1, C), F32),
        vmem((8, 1, C), F32),
        vmem((2, 1, C), F32),
        vmem((2, C), F32),
        vmem((NY - 1, 2, C), F32),
        vmem((NZ - 1, 2, C), F32),
        vmem((1, 2, C), F32),
        dma((5,)), dma((2, 3)), dma((2,)), dma((2,)), dma, dma((4, SUBS, 10)), dma((4,)), dma((4, SUBS)),
        dma((2,)), dma((2,)), dma((2,)), dma((2,)), dma((2,)), dma((2,)), dma((24,)), dma((24,)),
        dma((len(KEYS),)), dma((len(KEYS),)),
    ] + [vmem(PLAN[key], BF16) for key in KEYS]
    anywhere = pl.BlockSpec(memory_space=pl.ANY)
    in_vmem = pl.BlockSpec(memory_space=pltpu.VMEM)
    gw, gd = pl.pallas_call(
        kernel,
        out_shape=(jax.ShapeDtypeStruct((2, 16, C), BF16), jax.ShapeDtypeStruct((2, 16), F32)),
        in_specs=[anywhere] * 4,
        out_specs=(in_vmem, in_vmem),
        scratch_shapes=scratch,
        compiler_params=pltpu.CompilerParams(
            collective_id=0, has_side_effects=True, vmem_limit_bytes=60 * 2**20
        ),
        name="relay",
    )(
        currents.reshape(2, ROWS, C),
        weights.reshape(2, C, C),
        decay,
        out_grad.reshape(2, ROWS, C),
    )
    return gw[:, None], gd[:, None]


def solution(mesh):
    in_specs = (
        P(None, None, "dp", None),
        P(None, "section", None, None),
        P(None, "section", None),
        P(None, None, "dp", None),
    )
    out_specs = (P(None, "section", "dp", None), P(None, "section", "dp"))
    return jax.shard_map(on_device, mesh=mesh, in_specs=in_specs, out_specs=out_specs, check_vma=False)
```

```python
import functools
import itertools

import jax
import jax.numpy as jnp
from jax import lax
from jax.experimental import pallas as pl
from jax.experimental.pallas import tpu as pltpu
from jax.sharding import PartitionSpec as P

MESH = pl.DeviceIdType.MESH
F32 = jnp.float32
BF16 = jnp.bfloat16
C = 1024
ROWS = 256
HALF = 128
NY, NZ = 4, 8
GAIN = 4.0

SUBS = 2
WINDOW = 2
UNIT = 64 // SUBS
PLUS = ("y", "z", "y", "z", "xl", "xh", "xh", "xh")
MINUS = ("z", "y", "z", "y", "xl", "xh", "xh", "xh")
X, Y, Z, ZD, YD, XYD = "x", "y", "z", "zd", "yd", "xyd"

STREAMS = (
    (
        (0, 2, (Z, Y, X,), -1),
        (2, 2, (X, Y, ZD,), -1),
        (4, 2, (Z, XYD,), -1),
        (6, 1, (Y, Z, X,), 1),
        (7, 1, (X, Y, ZD,), -1),
    ),
    (
        (0, 2, (X, Y, Z,), 1),
        (2, 2, (Z, YD, X,), 1),
        (4, 2, (Y, Z, X,), -1),
        (6, 2, (Y, Z, X,), 1),
    ),
)
ORDER = (
    16, 17, -1, 18, 19, -1, -1, -1, 17, 17, -1, -1, -2, 0, 1, -1, 3, 18, 2, 4,
    17, 17, 16, 0, 19, 0, 2, -2, 3, 2, 17, 16, 0, 18, 0, 1, 2, 19, 2, 17,
    3, 0, 4, -2, 18, 18, 16, 1, 19, 2, 19, 17, 3, 3, 4, 16, 0, 19, 18, 18,
    16, 1, 17, 3, 16, 2, 19, 0, 3, -2, 19, 4, 16, 18, 3, 16, 1, 19, 0, 2,
    3, 16, 18, 4, 19, 0, 3, 18,
)
SIZES = {"x": 2, "y": NY, "z": NZ}


def offsets(stage):
    return [o for o in itertools.product(*[range(SIZES[axis]) for axis in stage.rstrip("d")]) if any(o)]


def hops_of(axis, way):
    far = SIZES[axis] // 2
    return {way: far, -way: far - 1}


def landing_plan():
    plan = {}
    for r in range(2):
        for s, (_, blocks, order, way) in enumerate(STREAMS[r]):
            span = dict(SIZES)
            for stage in order:
                for axis in stage.rstrip("d"):
                    span[axis] = 1
                shape = (blocks, span["x"], span["y"], span["z"], 16, 128)
                if stage in ("y", "z"):
                    for d, count in hops_of(stage, way).items():
                        for hop in range(1, count + 1):
                            plan[(r, s, stage, d, hop)] = shape
                else:
                    for offset in offsets(stage):
                        plan[(r, s, stage, offset)] = shape
    return plan


PLAN = landing_plan()
KEYS = list(PLAN)


def kernel(currents, weights, decay, out_grad, gw_ref, gd_ref, *scratch):
    (w, act, kept, gq, g, p_act, p_gq, part, dec, dd, dd_in, dv, dy, dz, dx) = scratch[:15]
    (l_sem, dec_sem, cw_s, cw_r, xh_s, pc_r, gs, half_r, pa_s, pa_r, pg_s, pg_r, dd_s, dd_r, dv_s, dv_r, rs_s, rs_r) = scratch[15:33]
    landing = dict(zip(KEYS, scratch[33:]))
    number = {key: i for i, key in enumerate(KEYS)}

    sec = lax.axis_index("section")
    dp = lax.axis_index("dp")
    xh, c = sec // 2, sec % 2
    xl, y, z = dp // 32, (dp // 8) % 4, dp % 8

    def device(xh=xh, c=c, xl=xl, y=y, z=z):
        return (xh * 2 + c, xl * 32 + y * 8 + z)

    core = device(c=1 - c)
    to_xl = device(xl=1 - xl)
    y_by = lambda k: device(y=(y + k) % NY)
    z_by = lambda k: device(z=(z + k) % NZ)
    across = lambda core_there: device(xh=1 - xh, xl=1 - xl, c=core_there)

    def remote(src, dst, send, recv, to):
        return pltpu.make_async_remote_copy(
            src_ref=src, dst_ref=dst, send_sem=send, recv_sem=recv, device_id=to, device_id_type=MESH
        )

    local = []
    for r in range(2):
        local.append(pltpu.make_async_copy(weights.at[r], w.at[r * 4 + sec], l_sem.at[r]))
    local.append(pltpu.make_async_copy(currents.at[c], act.at[0], l_sem.at[2]))
    local.append(pltpu.make_async_copy(out_grad.at[c], g, l_sem.at[3]))
    local.append(pltpu.make_async_copy(decay, dec.at[sec], l_sem.at[4]))
    for copy in local:
        copy.start()

    partners = [core, to_xl, across(c), across(1 - c)]
    partners += [y_by(k) for k in range(1, NY)] + [z_by(k) for k in range(1, NZ)]
    partners += [device(xl=1 - xl, y=(y + k) % NY) for k in range(1, NY)]
    barrier = pltpu.get_barrier_semaphore()
    for partner in partners:
        pl.semaphore_signal(barrier, inc=1, device_id=partner, device_id_type=MESH)
    pl.semaphore_wait(barrier, len(partners))

    colour_there = (4 * (1 - xl) + 2 * y + z) % 8
    colour = (4 * xl + 2 * y + z) % 8

    def rows_of(half, sub, unit):
        start = half * 512 + sub * (512 // SUBS) + (unit % 8) * UNIT
        return pl.ds(pl.multiple_of(start, 16), UNIT)

    dec_copies = []
    for i, to in enumerate((core, across(c), across(1 - c))):
        dec_copies.append(remote(decay, dec.at[sec], dec_sem.at[0, i], dec_sem.at[1, i], to))
    for copy in dec_copies:
        copy.start()

    def send_across(phase):
        if phase < 2:
            for half in range(2):
                rows = rows_of(half, phase, colour_there)
                remote(weights.at[0, rows], w.at[sec, rows], xh_s, pc_r.at[c, phase, 0], across(half)).start()
            return
        layer = 2 + xh * 2 + phase
        for sub in range(2):
            here = w.at[layer, rows_of(c, sub, colour_there)]
            remote(here, here, xh_s, pc_r.at[phase, sub, 0], across(c)).start()
        if phase == 3:
            for i in range(4, 8):
                for route, piece, unit in ((PLUS, 1, 3), (MINUS, 7, 5)):
                    if route[i] == "xh":
                        here = w.at[2 + xh * 2 + i // 2, rows_of(c, i % 2, colour_there + unit)]
                        remote(here, here, xh_s, pc_r.at[i // 2, i % 2, piece], across(c)).start()

    for phase in range(WINDOW):
        send_across(phase)
    remote(weights.at[0], w.at[sec], cw_s.at[0], cw_r.at[0], core).start()
    remote(weights.at[1], w.at[4 + sec], cw_s.at[1], cw_r.at[1], core).start()

    def layer_of(q):
        return (q // 2) * 4 + (1 - xh) * 2 + q % 2

    PIECES = (0, 3, 1, 7, 2, 6, 4, 5)

    def pass_on(q, sub, unit, piece, to):
        here = w.at[layer_of(q), rows_of(c, sub, colour + unit)]
        remote(here, here, gs.at[q], pc_r.at[q, sub, piece], to).start()

    def arrived(q, sub, piece):
        here = w.at[layer_of(q), rows_of(c, sub, colour + PIECES[piece])]
        pltpu.make_async_copy(here, here, pc_r.at[q, sub, piece]).wait()

    def both(phase):
        return ((0, phase), (1, phase)) if phase < 2 else ((phase, 0), (phase, 1))

    def first_hop(phase):
        for q, sub in both(phase):
            arrived(q, sub, 0)
            for piece, to in ((4, y_by(3)), (5, y_by(1)), (6, to_xl), (3, z_by(1)), (2, z_by(7))):
                pass_on(q, sub, 0, piece, to)
        if phase == 0:
            local[1].wait()
            pltpu.make_async_copy(w.at[4], w.at[4], cw_r.at[1]).wait()
        if phase + WINDOW < 2 * SUBS:
            send_across(phase + WINDOW)

    def second_hop(phase):
        for i, (q, sub) in enumerate(both(phase)):
            plus, minus = PLUS[phase * 2 + i], MINUS[phase * 2 + i]
            arrived(q, sub, 2)
            if plus == "y":
                pass_on(q, sub, 1, 1, y_by(3))
            if minus == "xl":
                pass_on(q, sub, 1, 7, to_xl)
            arrived(q, sub, 3)
            if minus == "y":
                pass_on(q, sub, 7, 7, y_by(1))
            if plus == "xl":
                pass_on(q, sub, 7, 1, to_xl)
            if plus == "z":
                arrived(q, sub, 4)
                pass_on(q, sub, 2, 1, z_by(7))
            if minus == "z":
                arrived(q, sub, 5)
                pass_on(q, sub, 6, 7, z_by(1))

    def rest(phase):
        for i, (q, sub) in enumerate(both(phase)):
            for piece in (4, 5, 6, 1, 7):
                if (piece == 4 and PLUS[phase * 2 + i] == "z") or (piece == 5 and MINUS[phase * 2 + i] == "z"):
                    continue
                arrived(q, sub, piece)
            start = c * 512 + sub * (512 // SUBS)
            here = w.at[layer_of(q), pl.ds(pl.multiple_of(start, 128), 512 // SUBS)]
            remote(here, here, gs.at[q], half_r.at[q, sub], core).start()

    def tile(j, size=256):
        return pl.ds(pl.multiple_of(j * size, size), size)

    def own_chip(layer):
        return (layer // 2) % 2 == xh

    def forward(layer):
        lap = layer // 4

        @pl.when(own_chip(layer) & (layer % 2 == c) & (lap == 0))
        def _():
            pltpu.make_async_copy(weights.at[0], w.at[layer], l_sem.at[0]).wait()

        @pl.when(own_chip(layer) & (layer % 2 != c) & (lap == 0))
        def _():
            pltpu.make_async_copy(w.at[layer], w.at[layer], cw_r.at[0]).wait()

        @pl.when(own_chip(layer) & (layer % 2 != c))
        def _():
            remote(act.at[layer], p_act.at[lap], pa_s.at[lap], pa_r.at[lap], core).start()

        @pl.when(jnp.logical_not(own_chip(layer)))
        def _():
            for sub in range(SUBS):
                start = (1 - c) * 512 + sub * (512 // SUBS)
                here = w.at[layer, pl.ds(pl.multiple_of(start, 128), 512 // SUBS)]
                pltpu.make_async_copy(here, here, half_r.at[lap * 2 + layer % 2, sub]).wait()

        @pl.loop(0, 4, unroll=True)
        def _(j):
            cols = tile(j)
            pre = jnp.dot(act[layer], w[layer, :, cols], preferred_element_type=F32)
            rate = dec[layer % 4, lap, :, cols]
            old = act[layer, :, cols].astype(F32)
            h0 = pre[:HALF]
            s0 = 1.0 / (1.0 + jnp.exp(-GAIN * (h0 - 1.0)))
            rest0 = 1.0 - s0
            v0 = h0 * rest0
            h1 = rate * v0 + pre[HALF:]
            s1 = 1.0 / (1.0 + jnp.exp(-GAIN * (h1 - 1.0)))
            slope0 = GAIN * s0 * rest0
            kept[layer, 0, :, cols] = slope0
            kept[layer, 1, :, cols] = GAIN * s1 * (1.0 - s1)
            kept[layer, 2, :, cols] = rate * (rest0 - h0 * slope0)
            kept[layer, 3, :, cols] = v0
            act[layer + 1, pl.ds(0, HALF), cols] = (old[:HALF] + s0).astype(BF16)
            act[layer + 1, pl.ds(HALF, HALF), cols] = (old[HALF:] + s1).astype(BF16)

    def backward(layer, with_input=True):
        lap = layer // 4

        @pl.loop(0, 4, unroll=True)
        def _(j):
            cols = tile(j)
            gh1 = g[pl.ds(HALF, HALF), cols].astype(F32) * kept[layer, 1, :, cols]
            gh0 = g[pl.ds(0, HALF), cols].astype(F32) * kept[layer, 0, :, cols] + gh1 * kept[layer, 2, :, cols]
            gq[layer, pl.ds(0, HALF), cols] = gh0.astype(BF16)
            gq[layer, pl.ds(HALF, HALF), cols] = gh1.astype(BF16)
            dd[layer, :, cols] = jnp.sum(gh1 * kept[layer, 3, :, cols], axis=0, keepdims=True)

        @pl.when(own_chip(layer) & (layer % 2 != c))
        def _():
            remote(gq.at[layer], p_gq.at[lap], pg_s.at[lap], pg_r.at[lap], core).start()
            remote(dd.at[layer], dd_in.at[lap], dd_s.at[lap], dd_r.at[lap], core).start()

        if with_input:

            @pl.loop(0, 4, unroll=True)
            def _(j):
                cols = tile(j)
                back = lax.dot_general(
                    gq[layer], w[layer, cols, :], (((1,), (1,)), ((), ())), preferred_element_type=F32
                )
                g[:, cols] = (g[:, cols].astype(F32) + back).astype(BF16)

    def weight_gradient(lap, n):
        layer = lap * 4 + sec
        if n == 0:
            pltpu.make_async_copy(p_act.at[lap], p_act.at[lap], pa_r.at[lap]).wait()
            pltpu.make_async_copy(p_gq.at[lap], p_gq.at[lap], pg_r.at[lap]).wait()
            pltpu.make_async_copy(dd_in.at[lap], dd_in.at[lap], dd_r.at[lap]).wait()
            dv[pl.ds(lap, 1), :] = dd[layer] + dd_in[lap]
        over_rows = (((0,), (0,)), ((), ()))
        cols = pl.ds(n * 512, 512)

        @pl.loop(0, 4, unroll=True)
        def _(i):
            total = lax.dot_general(
                act[layer, :, tile(i)], gq[layer, :, cols], over_rows, preferred_element_type=F32
            ) + lax.dot_general(
                p_act[lap, :, tile(i)], p_gq[lap, :, cols], over_rows, preferred_element_type=F32
            )
            for b in range(4):
                block = total[:, b * 128 : (b + 1) * 128].astype(BF16).reshape(2, 8, 16, 128)
                part[lap, n * 4 + b, i // 2, pl.ds((i % 2) * 2, 2)] = block

    sums = []

    def stream(r, s):
        first, blocks, order, way = STREAMS[r][s]
        where = {"x": pl.ds(0, 2), "y": pl.ds(0, NY), "z": pl.ds(0, NZ)}
        mine = {"x": xl, "y": y, "z": z}

        def chunk(places):
            at = {**where, **{axis: pl.ds(place, 1) for axis, place in places.items()}}
            return part.at[r, pl.ds(first, blocks), at["x"], at["y"], at["z"]]

        def send(places, key, to):
            i = number[key]
            copy = remote(chunk(places), landing[key], rs_s.at[i], rs_r.at[i], to)
            copy.start()
            sums.append(copy)

        def wait(key):
            i = number[key]
            pltpu.make_async_copy(landing[key], landing[key], rs_r.at[i]).wait()

        def own_sum(keys):
            for key in keys:
                wait(key)
            total = chunk({})[...].astype(F32)
            for key in keys:
                total = total + landing[key][...].astype(F32)
            return total

        pending = []
        for stage in order:
            if pending:
                chunk({})[...] = own_sum(pending).astype(BF16)
            if stage in ("y", "z"):
                n, me = SIZES[stage], mine[stage]
                by = y_by if stage == "y" else z_by
                hops = hops_of(stage, way)
                for d in (1, -1):
                    send({stage: (me + d * hops[d] + n) % n}, (r, s, stage, d, 1), by((d + n) % n))
                yield
                for hop in range(2, n // 2 + 1):
                    for d in (way, -way):
                        if hop > hops[d]:
                            continue
                        to = {stage: (me + d * (hops[d] - hop + 1) + n) % n}
                        came = (r, s, stage, d, hop - 1)
                        wait(came)
                        here = chunk(to)
                        here[...] = (here[...].astype(F32) + landing[came][...].astype(F32)).astype(BF16)
                        send(to, (r, s, stage, d, hop), by((d + n) % n))
                        yield
                pending = [(r, s, stage, d, hops[d]) for d in (1, -1)]
                where[stage] = pl.ds(me, 1)
            else:
                axes = stage.rstrip("d")
                pending = []
                for offset in offsets(stage):
                    to = {axis: (mine[axis] + by) % SIZES[axis] for axis, by in zip(axes, offset)}
                    names = {"x": "xl", "y": "y", "z": "z"}
                    send(to, (r, s, stage, offset), device(**{names[axis]: place for axis, place in to.items()}))
                    pending.append((r, s, stage, offset))
                yield
                for axis in axes:
                    where[axis] = pl.ds(mine[axis], 1)
        total = own_sum(pending).astype(BF16)
        for b in range(blocks):
            gw_ref[r, :, pl.ds((first + b) * 128, 128)] = total[b, 0, 0, 0]

    def decay_sum():
        for i, (buffer, by, n) in enumerate(((dy, y_by, NY), (dz, z_by, NZ), (dx, lambda k: to_xl, 2))):
            copies = []
            for k in range(1, n):
                copies.append(remote(dv, buffer.at[k - 1], dv_s.at[i * 8 + k], dv_r.at[i * 8 + k], by(k)))
                copies[-1].start()
            yield
            for copy in copies:
                copy.wait()
            total = dv[...]
            for k in range(n - 1):
                total = total + buffer[k]
            dv[...] = total
        gd_ref[...] = pltpu.roll(dv[...], (C - dp * 16) % C, axis=1)

    start = 2 - 2 * xh
    local[2].wait()
    local[4].wait()
    for copy in dec_copies:
        copy.wait_recv()

    def forward_loop(low, high):
        def body(layer, carry):
            forward(layer)
            return carry

        lax.fori_loop(low, high, body, 0)

    forward_loop(0, start)
    first_hop(0)
    first_hop(1)
    second_hop(0)
    first_hop(2)
    second_hop(1)
    rest(0)
    first_hop(3)
    second_hop(2)
    rest(1)
    forward(start)
    forward(start + 1)
    second_hop(3)
    rest(2)
    forward(start + 2)
    rest(3)
    forward_loop(start + 3, 8)

    local[3].wait()
    count = 4 - 2 * xh

    def body(i, carry):
        backward(7 - i)
        return carry

    lax.fori_loop(0, count, body, 0)
    weight_gradient(1, 0)
    pieces = [functools.partial(weight_gradient, 1, 1)]
    pieces += [functools.partial(backward, 7 - count - i, i < 3) for i in range(4)]
    pieces += [functools.partial(weight_gradient, 0, n) for n in range(2)]
    streams = {r * 16 + s: stream(r, s) for r in range(2) for s in range(len(STREAMS[r]))}
    streams[-2] = decay_sum()

    def advance(key):
        if key == -1:
            pieces.pop(0)()
        elif next(streams[key], 0) is not None:
            del streams[key]

    for key in ORDER:
        advance(key)
    assert not streams and not pieces

    for copy in sums:
        copy.wait_send()
    for copy in dec_copies:
        copy.wait_send()
    direct = sum(route[i] == "xh" for route in (PLUS, MINUS) for i in range(8))
    sent = w.at[0, pl.ds(0, (8 + direct) * UNIT)]
    pltpu.make_async_copy(sent, sent, xh_s).wait()
    for q in range(4):
        parts = (q, q + 2) if q < 2 else (2 * q, 2 * q + 1)
        passed = sum(5 + (PLUS[p] != "xh") + (MINUS[p] != "xh") for p in parts)
        sent = w.at[0, pl.ds(0, passed * UNIT + 512)]
        pltpu.make_async_copy(sent, sent, gs.at[q]).wait()
    for r in range(2):
        pltpu.make_async_copy(w.at[0], w.at[0], cw_s.at[r]).wait()
        pltpu.make_async_copy(p_act.at[r], p_act.at[r], pa_s.at[r]).wait()
        pltpu.make_async_copy(p_gq.at[r], p_gq.at[r], pg_s.at[r]).wait()
        pltpu.make_async_copy(dd_in.at[r], dd_in.at[r], dd_s.at[r]).wait()


def hand_on(gw_in, gd_in, gw_ref, gd_ref):
    gw_ref[...] = gw_in[...]
    gd_ref[...] = gd_in[:, :16]


def on_device(currents, weights, decay, out_grad):
    dma = pltpu.SemaphoreType.DMA
    vmem = pltpu.VMEM
    scratch = [
        vmem((8, C, C), BF16),
        vmem((9, ROWS, C), BF16),
        vmem((8, 4, HALF, C), F32),
        vmem((8, ROWS, C), BF16),
        vmem((ROWS, C), BF16),
        vmem((2, ROWS, C), BF16),
        vmem((2, ROWS, C), BF16),
        vmem((2, 8, 2, NY, NZ, 16, 128), BF16),
        vmem((4, 2, 1, C), F32),
        vmem((8, 1, C), F32),
        vmem((2, 1, C), F32),
        vmem((2, C), F32),
        vmem((NY - 1, 2, C), F32),
        vmem((NZ - 1, 2, C), F32),
        vmem((1, 2, C), F32),
        dma((5,)), dma((2, 3)), dma((2,)), dma((2,)), dma, dma((4, SUBS, 8)), dma((4,)), dma((4, SUBS)),
        dma((2,)), dma((2,)), dma((2,)), dma((2,)), dma((2,)), dma((2,)), dma((24,)), dma((24,)),
        dma((len(KEYS),)), dma((len(KEYS),)),
    ] + [vmem(PLAN[key], BF16) for key in KEYS]
    anywhere = pl.BlockSpec(memory_space=pl.ANY)
    in_vmem = pl.BlockSpec(memory_space=pltpu.VMEM)
    gw, gd = pl.pallas_call(
        kernel,
        out_shape=(jax.ShapeDtypeStruct((2, 16, C), BF16), jax.ShapeDtypeStruct((2, C), F32)),
        in_specs=[anywhere] * 4,
        out_specs=(in_vmem, in_vmem),
        scratch_shapes=scratch,
        compiler_params=pltpu.CompilerParams(
            collective_id=0, has_side_effects=True, vmem_limit_bytes=60 * 2**20
        ),
        name="relay",
    )(
        currents.reshape(2, ROWS, C),
        weights.reshape(2, C, C),
        decay,
        out_grad.reshape(2, ROWS, C),
    )
    gw, gd = pl.pallas_call(
        hand_on,
        out_shape=(jax.ShapeDtypeStruct((2, 16, C), BF16), jax.ShapeDtypeStruct((2, 16), F32)),
        in_specs=[in_vmem] * 2,
        out_specs=(in_vmem, in_vmem),
        name="results",
    )(gw, gd)
    return gw[:, None], gd[:, None]


def solution(mesh):
    in_specs = (
        P(None, None, "dp", None),
        P(None, "section", None, None),
        P(None, "section", None),
        P(None, None, "dp", None),
    )
    out_specs = (P(None, "section", "dp", None), P(None, "section", "dp"))
    return jax.shard_map(on_device, mesh=mesh, in_specs=in_specs, out_specs=out_specs, check_vma=False)
```

```python
import functools
import itertools

import jax
import jax.numpy as jnp
from jax import lax
from jax.experimental import pallas as pl
from jax.experimental.pallas import tpu as pltpu
from jax.sharding import PartitionSpec as P

MESH = pl.DeviceIdType.MESH
F32 = jnp.float32
BF16 = jnp.bfloat16
C = 1024
ROWS = 256
HALF = 128
NY, NZ = 4, 8
GAIN = 4.0

SUBS = 2
WINDOW = 2
UNIT = 64 // SUBS
PLUS = ("y", "z", "y", "z", "xl", "xh", "xh", "xh")
MINUS = ("z", "y", "z", "y", "xl", "xh", "xh", "xh")
X, Y, Z, ZD, YD, XYD = "x", "y", "z", "zd", "yd", "xyd"

STREAMS = (
    (
        (0, 2, (Z, Y, X,), -1),
        (2, 2, (X, Y, ZD,), -1),
        (4, 2, (Z, XYD,), -1),
        (6, 1, (Y, Z, X,), 1),
        (7, 1, (X, Y, ZD,), -1),
    ),
    (
        (0, 2, (X, Y, Z,), 1),
        (2, 2, (Z, YD, X,), 1),
        (4, 2, (Y, Z, X,), -1),
        (6, 2, (Y, Z, X,), 1),
    ),
)
ORDER = (
    16, 17, -1, 18, 19, -1, -1, -1, 17, 17, -1, -1, -2, 0, 1, -1, 3, 18, 2, 4,
    17, 17, 16, 0, 19, 0, 2, -2, 3, 2, 17, 16, 0, 18, 0, 1, 2, 19, 2, 17,
    3, 0, 4, -2, 18, 18, 16, 1, 19, 2, 19, 17, 3, 3, 4, 16, 0, 19, 18, 18,
    16, 1, 17, 3, 16, 2, 19, 0, 3, -2, 19, 4, 16, 18, 3, 16, 1, 19, 0, 2,
    3, 16, 18, 4, 19, 0, 3, 18,
)
SIZES = {"x": 2, "y": NY, "z": NZ}


def offsets(stage):
    return [o for o in itertools.product(*[range(SIZES[axis]) for axis in stage.rstrip("d")]) if any(o)]


def hops_of(axis, way):
    far = SIZES[axis] // 2
    return {way: far, -way: far - 1}


def landing_plan():
    plan = {}
    for r in range(2):
        for s, (_, blocks, order, way) in enumerate(STREAMS[r]):
            span = dict(SIZES)
            for stage in order:
                for axis in stage.rstrip("d"):
                    span[axis] = 1
                shape = (blocks, span["x"], span["y"], span["z"], 16, 128)
                if stage in ("y", "z"):
                    for d, count in hops_of(stage, way).items():
                        for hop in range(1, count + 1):
                            plan[(r, s, stage, d, hop)] = shape
                else:
                    for offset in offsets(stage):
                        plan[(r, s, stage, offset)] = shape
    return plan


PLAN = landing_plan()
KEYS = list(PLAN)


def kernel(currents, weights, decay, out_grad, gw_ref, gd_ref, *scratch):
    (w, act, kept, gq, g, p_act, p_gq, part, dec, dd, dd_in, dv, dy, dz, dx) = scratch[:15]
    (l_sem, dec_sem, cw_s, cw_r, xh_s, pc_r, gs, half_r, pa_s, pa_r, pg_s, pg_r, dd_s, dd_r, dv_s, dv_r, rs_s, rs_r) = scratch[15:33]
    landing = dict(zip(KEYS, scratch[33:]))
    number = {key: i for i, key in enumerate(KEYS)}

    sec = lax.axis_index("section")
    dp = lax.axis_index("dp")
    xh, c = sec // 2, sec % 2
    xl, y, z = dp // 32, (dp // 8) % 4, dp % 8

    def device(xh=xh, c=c, xl=xl, y=y, z=z):
        return (xh * 2 + c, xl * 32 + y * 8 + z)

    core = device(c=1 - c)
    to_xl = device(xl=1 - xl)
    y_by = lambda k: device(y=(y + k) % NY)
    z_by = lambda k: device(z=(z + k) % NZ)
    across = lambda core_there: device(xh=1 - xh, xl=1 - xl, c=core_there)

    def remote(src, dst, send, recv, to):
        return pltpu.make_async_remote_copy(
            src_ref=src, dst_ref=dst, send_sem=send, recv_sem=recv, device_id=to, device_id_type=MESH
        )

    local = []
    for r in range(2):
        local.append(pltpu.make_async_copy(weights.at[r], w.at[r * 4 + sec], l_sem.at[r]))
    local.append(pltpu.make_async_copy(currents.at[c], act.at[0], l_sem.at[2]))
    local.append(pltpu.make_async_copy(out_grad.at[c], g, l_sem.at[3]))
    local.append(pltpu.make_async_copy(decay, dec.at[sec], l_sem.at[4]))
    for copy in local:
        copy.start()

    partners = [core, to_xl, across(c), across(1 - c)]
    partners += [y_by(k) for k in range(1, NY)] + [z_by(k) for k in range(1, NZ)]
    partners += [device(xl=1 - xl, y=(y + k) % NY) for k in range(1, NY)]
    barrier = pltpu.get_barrier_semaphore()
    for partner in partners:
        pl.semaphore_signal(barrier, inc=1, device_id=partner, device_id_type=MESH)
    pl.semaphore_wait(barrier, len(partners))

    colour_there = (4 * (1 - xl) + 2 * y + z) % 8
    colour = (4 * xl + 2 * y + z) % 8

    def rows_of(half, sub, unit):
        start = half * 512 + sub * (512 // SUBS) + (unit % 8) * UNIT
        return pl.ds(pl.multiple_of(start, 16), UNIT)

    dec_copies = []
    for i, to in enumerate((core, across(c), across(1 - c))):
        dec_copies.append(remote(decay, dec.at[sec], dec_sem.at[0, i], dec_sem.at[1, i], to))
    for copy in dec_copies:
        copy.start()

    def send_across(phase):
        if phase < 2:
            for half in range(2):
                rows = rows_of(half, phase, colour_there)
                remote(weights.at[0, rows], w.at[sec, rows], xh_s, pc_r.at[c, phase, 0], across(half)).start()
            return
        layer = 2 + xh * 2 + phase
        for sub in range(2):
            here = w.at[layer, rows_of(c, sub, colour_there)]
            remote(here, here, xh_s, pc_r.at[phase, sub, 0], across(c)).start()
        if phase == 3:
            for i in range(4, 8):
                for route, piece, unit in ((PLUS, 1, 3), (MINUS, 7, 5)):
                    if route[i] == "xh":
                        here = w.at[2 + xh * 2 + i // 2, rows_of(c, i % 2, colour_there + unit)]
                        remote(here, here, xh_s, pc_r.at[i // 2, i % 2, piece], across(c)).start()

    for phase in range(WINDOW):
        send_across(phase)
    remote(weights.at[0], w.at[sec], cw_s.at[0], cw_r.at[0], core).start()
    remote(weights.at[1], w.at[4 + sec], cw_s.at[1], cw_r.at[1], core).start()

    def layer_of(q):
        return (q // 2) * 4 + (1 - xh) * 2 + q % 2

    PIECES = (0, 3, 1, 7, 2, 6, 4, 5)

    def pass_on(q, sub, unit, piece, to):
        here = w.at[layer_of(q), rows_of(c, sub, colour + unit)]
        remote(here, here, gs.at[q], pc_r.at[q, sub, piece], to).start()

    def arrived(q, sub, piece):
        here = w.at[layer_of(q), rows_of(c, sub, colour + PIECES[piece])]
        pltpu.make_async_copy(here, here, pc_r.at[q, sub, piece]).wait()

    def both(phase):
        return ((0, phase), (1, phase)) if phase < 2 else ((phase, 0), (phase, 1))

    def first_hop(phase):
        for q, sub in both(phase):
            arrived(q, sub, 0)
            for piece, to in ((4, y_by(3)), (5, y_by(1)), (6, to_xl), (3, z_by(1)), (2, z_by(7))):
                pass_on(q, sub, 0, piece, to)
        if phase == 0:
            local[1].wait()
            pltpu.make_async_copy(w.at[4], w.at[4], cw_r.at[1]).wait()
        if phase + WINDOW < 2 * SUBS:
            send_across(phase + WINDOW)

    def second_hop(phase):
        for i, (q, sub) in enumerate(both(phase)):
            plus, minus = PLUS[phase * 2 + i], MINUS[phase * 2 + i]
            arrived(q, sub, 2)
            if plus == "y":
                pass_on(q, sub, 1, 1, y_by(3))
            if minus == "xl":
                pass_on(q, sub, 1, 7, to_xl)
            arrived(q, sub, 3)
            if minus == "y":
                pass_on(q, sub, 7, 7, y_by(1))
            if plus == "xl":
                pass_on(q, sub, 7, 1, to_xl)
            if plus == "z":
                arrived(q, sub, 4)
                pass_on(q, sub, 2, 1, z_by(7))
            if minus == "z":
                arrived(q, sub, 5)
                pass_on(q, sub, 6, 7, z_by(1))

    def rest(phase):
        for i, (q, sub) in enumerate(both(phase)):
            for piece in (4, 5, 6, 1, 7):
                if (piece == 4 and PLUS[phase * 2 + i] == "z") or (piece == 5 and MINUS[phase * 2 + i] == "z"):
                    continue
                arrived(q, sub, piece)
            start = c * 512 + sub * (512 // SUBS)
            here = w.at[layer_of(q), pl.ds(pl.multiple_of(start, 128), 512 // SUBS)]
            remote(here, here, gs.at[q], half_r.at[q, sub], core).start()

    def tile(j, size=256):
        return pl.ds(pl.multiple_of(j * size, size), size)

    def own_chip(layer):
        return (layer // 2) % 2 == xh

    def forward(layer):
        lap = layer // 4

        @pl.when(own_chip(layer) & (layer % 2 == c) & (lap == 0))
        def _():
            pltpu.make_async_copy(weights.at[0], w.at[layer], l_sem.at[0]).wait()

        @pl.when(own_chip(layer) & (layer % 2 != c) & (lap == 0))
        def _():
            pltpu.make_async_copy(w.at[layer], w.at[layer], cw_r.at[0]).wait()

        @pl.when(own_chip(layer) & (layer % 2 != c))
        def _():
            remote(act.at[layer], p_act.at[lap], pa_s.at[lap], pa_r.at[lap], core).start()

        @pl.when(jnp.logical_not(own_chip(layer)))
        def _():
            for sub in range(SUBS):
                start = (1 - c) * 512 + sub * (512 // SUBS)
                here = w.at[layer, pl.ds(pl.multiple_of(start, 128), 512 // SUBS)]
                pltpu.make_async_copy(here, here, half_r.at[lap * 2 + layer % 2, sub]).wait()

        @pl.loop(0, 2, unroll=True)
        def _(j):
            cols = tile(j, 512)
            pre = jnp.dot(act[layer], w[layer, :, cols], preferred_element_type=F32)
            rate = dec[layer % 4, lap, :, cols]
            old = act[layer, :, cols].astype(F32)
            h0 = pre[:HALF]
            s0 = 1.0 / (1.0 + jnp.exp(-GAIN * (h0 - 1.0)))
            rest0 = 1.0 - s0
            v0 = h0 * rest0
            h1 = rate * v0 + pre[HALF:]
            s1 = 1.0 / (1.0 + jnp.exp(-GAIN * (h1 - 1.0)))
            slope0 = GAIN * s0 * rest0
            kept[layer, 0, :, cols] = slope0
            kept[layer, 1, :, cols] = GAIN * s1 * (1.0 - s1)
            kept[layer, 2, :, cols] = rate * (rest0 - h0 * slope0)
            kept[layer, 3, :, cols] = v0
            act[layer + 1, pl.ds(0, HALF), cols] = (old[:HALF] + s0).astype(BF16)
            act[layer + 1, pl.ds(HALF, HALF), cols] = (old[HALF:] + s1).astype(BF16)

    def backward(layer, with_input=True):
        lap = layer // 4

        @pl.loop(0, 4, unroll=True)
        def _(j):
            cols = tile(j)
            gh1 = g[pl.ds(HALF, HALF), cols].astype(F32) * kept[layer, 1, :, cols]
            gh0 = g[pl.ds(0, HALF), cols].astype(F32) * kept[layer, 0, :, cols] + gh1 * kept[layer, 2, :, cols]
            gq[layer, pl.ds(0, HALF), cols] = gh0.astype(BF16)
            gq[layer, pl.ds(HALF, HALF), cols] = gh1.astype(BF16)
            dd[layer, :, cols] = jnp.sum(gh1 * kept[layer, 3, :, cols], axis=0, keepdims=True)

        @pl.when(own_chip(layer) & (layer % 2 != c))
        def _():
            remote(gq.at[layer], p_gq.at[lap], pg_s.at[lap], pg_r.at[lap], core).start()
            remote(dd.at[layer], dd_in.at[lap], dd_s.at[lap], dd_r.at[lap], core).start()

        if with_input:

            @pl.loop(0, 4, unroll=True)
            def _(j):
                cols = tile(j)
                back = lax.dot_general(
                    gq[layer], w[layer, cols, :], (((1,), (1,)), ((), ())), preferred_element_type=F32
                )
                g[:, cols] = (g[:, cols].astype(F32) + back).astype(BF16)

    def weight_gradient(lap, n):
        layer = lap * 4 + sec
        if n == 0:
            pltpu.make_async_copy(p_act.at[lap], p_act.at[lap], pa_r.at[lap]).wait()
            pltpu.make_async_copy(p_gq.at[lap], p_gq.at[lap], pg_r.at[lap]).wait()
            pltpu.make_async_copy(dd_in.at[lap], dd_in.at[lap], dd_r.at[lap]).wait()
            dv[pl.ds(lap, 1), :] = dd[layer] + dd_in[lap]
        over_rows = (((0,), (0,)), ((), ()))
        cols = pl.ds(n * 512, 512)

        @pl.loop(0, 4, unroll=True)
        def _(i):
            total = lax.dot_general(
                act[layer, :, tile(i)], gq[layer, :, cols], over_rows, preferred_element_type=F32
            ) + lax.dot_general(
                p_act[lap, :, tile(i)], p_gq[lap, :, cols], over_rows, preferred_element_type=F32
            )
            for b in range(4):
                block = total[:, b * 128 : (b + 1) * 128].astype(BF16).reshape(2, 8, 16, 128)
                part[lap, n * 4 + b, i // 2, pl.ds((i % 2) * 2, 2)] = block

    sums = []

    def stream(r, s):
        first, blocks, order, way = STREAMS[r][s]
        where = {"x": pl.ds(0, 2), "y": pl.ds(0, NY), "z": pl.ds(0, NZ)}
        mine = {"x": xl, "y": y, "z": z}

        def chunk(places):
            at = {**where, **{axis: pl.ds(place, 1) for axis, place in places.items()}}
            return part.at[r, pl.ds(first, blocks), at["x"], at["y"], at["z"]]

        def send(places, key, to):
            i = number[key]
            copy = remote(chunk(places), landing[key], rs_s.at[i], rs_r.at[i], to)
            copy.start()
            sums.append(copy)

        def wait(key):
            i = number[key]
            pltpu.make_async_copy(landing[key], landing[key], rs_r.at[i]).wait()

        def own_sum(keys):
            for key in keys:
                wait(key)
            total = chunk({})[...].astype(F32)
            for key in keys:
                total = total + landing[key][...].astype(F32)
            return total

        pending = []
        for stage in order:
            if pending:
                chunk({})[...] = own_sum(pending).astype(BF16)
            if stage in ("y", "z"):
                n, me = SIZES[stage], mine[stage]
                by = y_by if stage == "y" else z_by
                hops = hops_of(stage, way)
                for d in (1, -1):
                    send({stage: (me + d * hops[d] + n) % n}, (r, s, stage, d, 1), by((d + n) % n))
                yield
                for hop in range(2, n // 2 + 1):
                    for d in (way, -way):
                        if hop > hops[d]:
                            continue
                        to = {stage: (me + d * (hops[d] - hop + 1) + n) % n}
                        came = (r, s, stage, d, hop - 1)
                        wait(came)
                        here = chunk(to)
                        here[...] = (here[...].astype(F32) + landing[came][...].astype(F32)).astype(BF16)
                        send(to, (r, s, stage, d, hop), by((d + n) % n))
                        yield
                pending = [(r, s, stage, d, hops[d]) for d in (1, -1)]
                where[stage] = pl.ds(me, 1)
            else:
                axes = stage.rstrip("d")
                pending = []
                for offset in offsets(stage):
                    to = {axis: (mine[axis] + by) % SIZES[axis] for axis, by in zip(axes, offset)}
                    names = {"x": "xl", "y": "y", "z": "z"}
                    send(to, (r, s, stage, offset), device(**{names[axis]: place for axis, place in to.items()}))
                    pending.append((r, s, stage, offset))
                yield
                for axis in axes:
                    where[axis] = pl.ds(mine[axis], 1)
        total = own_sum(pending).astype(BF16)
        for b in range(blocks):
            gw_ref[r, :, pl.ds((first + b) * 128, 128)] = total[b, 0, 0, 0]

    def decay_sum():
        for i, (buffer, by, n) in enumerate(((dy, y_by, NY), (dz, z_by, NZ), (dx, lambda k: to_xl, 2))):
            copies = []
            for k in range(1, n):
                copies.append(remote(dv, buffer.at[k - 1], dv_s.at[i * 8 + k], dv_r.at[i * 8 + k], by(k)))
                copies[-1].start()
            yield
            for copy in copies:
                copy.wait()
            total = dv[...]
            for k in range(n - 1):
                total = total + buffer[k]
            dv[...] = total
        gd_ref[...] = pltpu.roll(dv[...], (C - dp * 16) % C, axis=1)

    start = 2 - 2 * xh
    local[2].wait()
    local[4].wait()
    for copy in dec_copies:
        copy.wait_recv()

    def forward_loop(low, high):
        def body(layer, carry):
            forward(layer)
            return carry

        lax.fori_loop(low, high, body, 0)

    forward_loop(0, start)
    first_hop(0)
    first_hop(1)
    second_hop(0)
    first_hop(2)
    second_hop(1)
    rest(0)
    first_hop(3)
    second_hop(2)
    rest(1)
    forward(start)
    forward(start + 1)
    second_hop(3)
    rest(2)
    forward(start + 2)
    rest(3)
    forward_loop(start + 3, 8)

    local[3].wait()
    count = 4 - 2 * xh

    def body(i, carry):
        backward(7 - i)
        return carry

    lax.fori_loop(0, count, body, 0)
    weight_gradient(1, 0)
    pieces = [functools.partial(weight_gradient, 1, 1)]
    pieces += [functools.partial(backward, 7 - count - i, i < 3) for i in range(4)]
    pieces += [functools.partial(weight_gradient, 0, n) for n in range(2)]
    streams = {r * 16 + s: stream(r, s) for r in range(2) for s in range(len(STREAMS[r]))}
    streams[-2] = decay_sum()

    def advance(key):
        if key == -1:
            pieces.pop(0)()
        elif next(streams[key], 0) is not None:
            del streams[key]

    for key in ORDER:
        advance(key)
    assert not streams and not pieces

    for copy in sums:
        copy.wait_send()
    for copy in dec_copies:
        copy.wait_send()
    direct = sum(route[i] == "xh" for route in (PLUS, MINUS) for i in range(8))
    sent = w.at[0, pl.ds(0, (8 + direct) * UNIT)]
    pltpu.make_async_copy(sent, sent, xh_s).wait()
    for q in range(4):
        parts = (q, q + 2) if q < 2 else (2 * q, 2 * q + 1)
        passed = sum(5 + (PLUS[p] != "xh") + (MINUS[p] != "xh") for p in parts)
        sent = w.at[0, pl.ds(0, passed * UNIT + 512)]
        pltpu.make_async_copy(sent, sent, gs.at[q]).wait()
    for r in range(2):
        pltpu.make_async_copy(w.at[0], w.at[0], cw_s.at[r]).wait()
        pltpu.make_async_copy(p_act.at[r], p_act.at[r], pa_s.at[r]).wait()
        pltpu.make_async_copy(p_gq.at[r], p_gq.at[r], pg_s.at[r]).wait()
        pltpu.make_async_copy(dd_in.at[r], dd_in.at[r], dd_s.at[r]).wait()


def hand_on(gw_in, gd_in, gw_ref, gd_ref):
    gw_ref[...] = gw_in[...]
    gd_ref[...] = gd_in[:, :16]


def on_device(currents, weights, decay, out_grad):
    dma = pltpu.SemaphoreType.DMA
    vmem = pltpu.VMEM
    scratch = [
        vmem((8, C, C), BF16),
        vmem((9, ROWS, C), BF16),
        vmem((8, 4, HALF, C), F32),
        vmem((8, ROWS, C), BF16),
        vmem((ROWS, C), BF16),
        vmem((2, ROWS, C), BF16),
        vmem((2, ROWS, C), BF16),
        vmem((2, 8, 2, NY, NZ, 16, 128), BF16),
        vmem((4, 2, 1, C), F32),
        vmem((8, 1, C), F32),
        vmem((2, 1, C), F32),
        vmem((2, C), F32),
        vmem((NY - 1, 2, C), F32),
        vmem((NZ - 1, 2, C), F32),
        vmem((1, 2, C), F32),
        dma((5,)), dma((2, 3)), dma((2,)), dma((2,)), dma, dma((4, SUBS, 8)), dma((4,)), dma((4, SUBS)),
        dma((2,)), dma((2,)), dma((2,)), dma((2,)), dma((2,)), dma((2,)), dma((24,)), dma((24,)),
        dma((len(KEYS),)), dma((len(KEYS),)),
    ] + [vmem(PLAN[key], BF16) for key in KEYS]
    anywhere = pl.BlockSpec(memory_space=pl.ANY)
    in_vmem = pl.BlockSpec(memory_space=pltpu.VMEM)
    gw, gd = pl.pallas_call(
        kernel,
        out_shape=(jax.ShapeDtypeStruct((2, 16, C), BF16), jax.ShapeDtypeStruct((2, C), F32)),
        in_specs=[anywhere] * 4,
        out_specs=(in_vmem, in_vmem),
        scratch_shapes=scratch,
        compiler_params=pltpu.CompilerParams(
            collective_id=0, has_side_effects=True, vmem_limit_bytes=60 * 2**20
        ),
        name="relay",
    )(
        currents.reshape(2, ROWS, C),
        weights.reshape(2, C, C),
        decay,
        out_grad.reshape(2, ROWS, C),
    )
    gw, gd = pl.pallas_call(
        hand_on,
        out_shape=(jax.ShapeDtypeStruct((2, 16, C), BF16), jax.ShapeDtypeStruct((2, 16), F32)),
        in_specs=[in_vmem] * 2,
        out_specs=(in_vmem, in_vmem),
        name="results",
    )(gw, gd)
    return gw[:, None], gd[:, None]


def solution(mesh):
    in_specs = (
        P(None, None, "dp", None),
        P(None, "section", None, None),
        P(None, "section", None),
        P(None, None, "dp", None),
    )
    out_specs = (P(None, "section", "dp", None), P(None, "section", "dp"))
    return jax.shard_map(on_device, mesh=mesh, in_specs=in_specs, out_specs=out_specs, check_vma=False)
```

```python
import functools
import itertools

import jax
import jax.numpy as jnp
from jax import lax
from jax.experimental import pallas as pl
from jax.experimental.pallas import tpu as pltpu
from jax.sharding import PartitionSpec as P

MESH = pl.DeviceIdType.MESH
F32 = jnp.float32
BF16 = jnp.bfloat16
C = 1024
ROWS = 256
HALF = 128
NY, NZ = 4, 8
GAIN = 4.0

SUBS = 2
WINDOW = 2
UNIT = 64 // SUBS
PLUS = ("y", "z", "y", "z", "xl", "xh", "xh", "xh")
MINUS = ("z", "y", "z", "y", "xl", "xh", "xh", "xh")
X, Y, Z, ZD, YD, XYD = "x", "y", "z", "zd", "yd", "xyd"

STREAMS = (
    (
        (0, 2, (Z, Y, X,), -1),
        (2, 2, (X, Y, ZD,), -1),
        (4, 2, (Z, XYD,), -1),
        (6, 1, (Y, Z, X,), 1),
        (7, 1, (X, Y, ZD,), -1),
    ),
    (
        (0, 2, (X, Y, Z,), 1),
        (2, 2, (Z, YD, X,), 1),
        (4, 2, (Y, Z, X,), -1),
        (6, 2, (Y, Z, X,), 1),
    ),
)
ORDER = (
    16, 17, -1, 18, 19, -1, -1, -1, 17, 17, -1, -1, -2, 0, 1, -1, 3, 18, 2, 4,
    17, 17, 16, 0, 19, 0, 2, -2, 3, 2, 17, 16, 0, 18, 0, 1, 2, 19, 2, 17,
    3, 0, 4, -2, 18, 18, 16, 1, 19, 2, 19, 17, 3, 3, 4, 16, 0, 19, 18, 18,
    16, 1, 17, 3, 16, 2, 19, 0, 3, -2, 19, 4, 16, 18, 3, 16, 1, 19, 0, 2,
    3, 16, 18, 4, 19, 0, 3, 18,
)
SIZES = {"x": 2, "y": NY, "z": NZ}


def offsets(stage):
    return [o for o in itertools.product(*[range(SIZES[axis]) for axis in stage.rstrip("d")]) if any(o)]


def hops_of(axis, way):
    far = SIZES[axis] // 2
    return {way: far, -way: far - 1}


def landing_plan():
    plan = {}
    for r in range(2):
        for s, (_, blocks, order, way) in enumerate(STREAMS[r]):
            span = dict(SIZES)
            for stage in order:
                for axis in stage.rstrip("d"):
                    span[axis] = 1
                shape = (blocks, span["x"], span["y"], span["z"], 16, 128)
                if stage in ("y", "z"):
                    for d, count in hops_of(stage, way).items():
                        for hop in range(1, count + 1):
                            plan[(r, s, stage, d, hop)] = shape
                else:
                    for offset in offsets(stage):
                        plan[(r, s, stage, offset)] = shape
    return plan


PLAN = landing_plan()
KEYS = list(PLAN)


def kernel(currents, weights, decay, out_grad, gw_ref, gd_ref, *scratch):
    (w, act, kept, gq, g, p_act, p_gq, part, dec, dd, dd_in, dv, dy, dz, dx) = scratch[:15]
    (l_sem, dec_sem, cw_s, cw_r, xh_s, pc_r, gs, half_r, pa_s, pa_r, pg_s, pg_r, dd_s, dd_r, dv_s, dv_r, rs_s, rs_r) = scratch[15:33]
    landing = dict(zip(KEYS, scratch[33:]))
    number = {key: i for i, key in enumerate(KEYS)}

    sec = lax.axis_index("section")
    dp = lax.axis_index("dp")
    xh, c = sec // 2, sec % 2
    xl, y, z = dp // 32, (dp // 8) % 4, dp % 8

    def device(xh=xh, c=c, xl=xl, y=y, z=z):
        return (xh * 2 + c, xl * 32 + y * 8 + z)

    core = device(c=1 - c)
    to_xl = device(xl=1 - xl)
    y_by = lambda k: device(y=(y + k) % NY)
    z_by = lambda k: device(z=(z + k) % NZ)
    across = lambda core_there: device(xh=1 - xh, xl=1 - xl, c=core_there)

    def remote(src, dst, send, recv, to):
        return pltpu.make_async_remote_copy(
            src_ref=src, dst_ref=dst, send_sem=send, recv_sem=recv, device_id=to, device_id_type=MESH
        )

    local = []
    for r in range(2):
        local.append(pltpu.make_async_copy(weights.at[r], w.at[r * 4 + sec], l_sem.at[r]))
    local.append(pltpu.make_async_copy(currents.at[c], act.at[0], l_sem.at[2]))
    local.append(pltpu.make_async_copy(out_grad.at[c], g, l_sem.at[3]))
    local.append(pltpu.make_async_copy(decay, dec.at[sec], l_sem.at[4]))
    for copy in local:
        copy.start()

    partners = [core, to_xl, across(c), across(1 - c)]
    partners += [y_by(k) for k in range(1, NY)] + [z_by(k) for k in range(1, NZ)]
    partners += [device(xl=1 - xl, y=(y + k) % NY) for k in range(1, NY)]
    barrier = pltpu.get_barrier_semaphore()
    for partner in partners:
        pl.semaphore_signal(barrier, inc=1, device_id=partner, device_id_type=MESH)
    pl.semaphore_wait(barrier, len(partners))

    colour_there = (4 * (1 - xl) + 2 * y + z) % 8
    colour = (4 * xl + 2 * y + z) % 8

    def rows_of(half, sub, unit):
        start = half * 512 + sub * (512 // SUBS) + (unit % 8) * UNIT
        return pl.ds(pl.multiple_of(start, 16), UNIT)

    dec_copies = []
    for i, to in enumerate((core, across(c), across(1 - c))):
        dec_copies.append(remote(decay, dec.at[sec], dec_sem.at[0, i], dec_sem.at[1, i], to))
    for copy in dec_copies:
        copy.start()

    def send_across(phase):
        if phase < 2:
            for half in range(2):
                rows = rows_of(half, phase, colour_there)
                remote(weights.at[0, rows], w.at[sec, rows], xh_s, pc_r.at[c, phase, 0], across(half)).start()
            return
        layer = 2 + xh * 2 + phase
        for sub in range(2):
            here = w.at[layer, rows_of(c, sub, colour_there)]
            remote(here, here, xh_s, pc_r.at[phase, sub, 0], across(c)).start()
        if phase == 3:
            for i in range(4, 8):
                for route, piece, unit in ((PLUS, 1, 3), (MINUS, 7, 5)):
                    if route[i] == "xh":
                        here = w.at[2 + xh * 2 + i // 2, rows_of(c, i % 2, colour_there + unit)]
                        remote(here, here, xh_s, pc_r.at[i // 2, i % 2, piece], across(c)).start()

    for phase in range(WINDOW):
        send_across(phase)
    remote(weights.at[0], w.at[sec], cw_s.at[0], cw_r.at[0], core).start()
    remote(weights.at[1], w.at[4 + sec], cw_s.at[1], cw_r.at[1], core).start()

    def layer_of(q):
        return (q // 2) * 4 + (1 - xh) * 2 + q % 2

    PIECES = (0, 3, 1, 7, 2, 6, 4, 5)

    def pass_on(q, sub, unit, piece, to):
        here = w.at[layer_of(q), rows_of(c, sub, colour + unit)]
        remote(here, here, gs.at[q], pc_r.at[q, sub, piece], to).start()

    def arrived(q, sub, piece):
        here = w.at[layer_of(q), rows_of(c, sub, colour + PIECES[piece])]
        pltpu.make_async_copy(here, here, pc_r.at[q, sub, piece]).wait()

    def both(phase):
        return ((0, phase), (1, phase)) if phase < 2 else ((phase, 0), (phase, 1))

    def first_hop(phase):
        for q, sub in both(phase):
            arrived(q, sub, 0)
            for piece, to in ((4, y_by(3)), (5, y_by(1)), (6, to_xl), (3, z_by(1)), (2, z_by(7))):
                pass_on(q, sub, 0, piece, to)
        if phase == 0:
            local[1].wait()
            pltpu.make_async_copy(w.at[4], w.at[4], cw_r.at[1]).wait()
        if phase + WINDOW < 2 * SUBS:
            send_across(phase + WINDOW)

    def second_hop(phase):
        for i, (q, sub) in enumerate(both(phase)):
            plus, minus = PLUS[phase * 2 + i], MINUS[phase * 2 + i]
            arrived(q, sub, 2)
            if plus == "y":
                pass_on(q, sub, 1, 1, y_by(3))
            if minus == "xl":
                pass_on(q, sub, 1, 7, to_xl)
            arrived(q, sub, 3)
            if minus == "y":
                pass_on(q, sub, 7, 7, y_by(1))
            if plus == "xl":
                pass_on(q, sub, 7, 1, to_xl)
            if plus == "z":
                arrived(q, sub, 4)
                pass_on(q, sub, 2, 1, z_by(7))
            if minus == "z":
                arrived(q, sub, 5)
                pass_on(q, sub, 6, 7, z_by(1))

    def rest(phase):
        for i, (q, sub) in enumerate(both(phase)):
            for piece in (4, 5, 6, 1, 7):
                if (piece == 4 and PLUS[phase * 2 + i] == "z") or (piece == 5 and MINUS[phase * 2 + i] == "z"):
                    continue
                arrived(q, sub, piece)
            start = c * 512 + sub * (512 // SUBS)
            here = w.at[layer_of(q), pl.ds(pl.multiple_of(start, 128), 512 // SUBS)]
            remote(here, here, gs.at[q], half_r.at[q, sub], core).start()

    def tile(j, size=256):
        return pl.ds(pl.multiple_of(j * size, size), size)

    def own_chip(layer):
        return (layer // 2) % 2 == xh

    def forward(layer):
        lap = layer // 4

        @pl.when(own_chip(layer) & (layer % 2 == c) & (lap == 0))
        def _():
            pltpu.make_async_copy(weights.at[0], w.at[layer], l_sem.at[0]).wait()

        @pl.when(own_chip(layer) & (layer % 2 != c) & (lap == 0))
        def _():
            pltpu.make_async_copy(w.at[layer], w.at[layer], cw_r.at[0]).wait()

        @pl.when(own_chip(layer) & (layer % 2 != c))
        def _():
            remote(act.at[layer], p_act.at[lap], pa_s.at[lap], pa_r.at[lap], core).start()

        @pl.when(jnp.logical_not(own_chip(layer)))
        def _():
            for sub in range(SUBS):
                start = (1 - c) * 512 + sub * (512 // SUBS)
                here = w.at[layer, pl.ds(pl.multiple_of(start, 128), 512 // SUBS)]
                pltpu.make_async_copy(here, here, half_r.at[lap * 2 + layer % 2, sub]).wait()

        @pl.loop(0, 2, unroll=True)
        def _(j):
            cols = tile(j, 512)
            pre = jnp.dot(act[layer], w[layer, :, cols], preferred_element_type=F32)
            rate = dec[layer % 4, lap, :, cols]
            old = act[layer, :, cols].astype(F32)
            h0 = pre[:HALF]
            s0 = 1.0 / (1.0 + jnp.exp(-GAIN * (h0 - 1.0)))
            rest0 = 1.0 - s0
            v0 = h0 * rest0
            h1 = rate * v0 + pre[HALF:]
            s1 = 1.0 / (1.0 + jnp.exp(-GAIN * (h1 - 1.0)))
            slope0 = GAIN * s0 * rest0
            kept[layer, 0, :, cols] = slope0
            kept[layer, 1, :, cols] = GAIN * s1 * (1.0 - s1)
            kept[layer, 2, :, cols] = rate * (rest0 - h0 * slope0)
            kept[layer, 3, :, cols] = v0
            act[layer + 1, pl.ds(0, HALF), cols] = (old[:HALF] + s0).astype(BF16)
            act[layer + 1, pl.ds(HALF, HALF), cols] = (old[HALF:] + s1).astype(BF16)

    def backward(layer, with_input=True):
        lap = layer // 4

        @pl.loop(0, 4, unroll=True)
        def _(j):
            cols = tile(j)
            gh1 = g[pl.ds(HALF, HALF), cols].astype(F32) * kept[layer, 1, :, cols]
            gh0 = g[pl.ds(0, HALF), cols].astype(F32) * kept[layer, 0, :, cols] + gh1 * kept[layer, 2, :, cols]
            gq[layer, pl.ds(0, HALF), cols] = gh0.astype(BF16)
            gq[layer, pl.ds(HALF, HALF), cols] = gh1.astype(BF16)
            dd[layer, :, cols] = jnp.sum(gh1 * kept[layer, 3, :, cols], axis=0, keepdims=True)

        @pl.when(own_chip(layer) & (layer % 2 != c))
        def _():
            remote(gq.at[layer], p_gq.at[lap], pg_s.at[lap], pg_r.at[lap], core).start()
            remote(dd.at[layer], dd_in.at[lap], dd_s.at[lap], dd_r.at[lap], core).start()

        if with_input:

            @pl.loop(0, 4, unroll=True)
            def _(j):
                cols = tile(j)
                back = lax.dot_general(
                    gq[layer], w[layer, cols, :], (((1,), (1,)), ((), ())), preferred_element_type=F32
                )
                g[:, cols] = (g[:, cols].astype(F32) + back).astype(BF16)

    def weight_gradient(lap, n):
        layer = lap * 4 + sec
        if n == 0:
            pltpu.make_async_copy(p_act.at[lap], p_act.at[lap], pa_r.at[lap]).wait()
            pltpu.make_async_copy(p_gq.at[lap], p_gq.at[lap], pg_r.at[lap]).wait()
            pltpu.make_async_copy(dd_in.at[lap], dd_in.at[lap], dd_r.at[lap]).wait()
            dv[pl.ds(lap, 1), :] = dd[layer] + dd_in[lap]
        over_rows = (((0,), (0,)), ((), ()))
        cols = pl.ds(n * 512, 512)

        @pl.loop(0, 2, unroll=True)
        def _(i):
            total = lax.dot_general(
                act[layer, :, tile(i, 512)], gq[layer, :, cols], over_rows, preferred_element_type=F32
            ) + lax.dot_general(
                p_act[lap, :, tile(i, 512)], p_gq[lap, :, cols], over_rows, preferred_element_type=F32
            )
            for b in range(4):
                block = total[:, b * 128 : (b + 1) * 128].astype(BF16).reshape(4, 8, 16, 128)
                part[lap, n * 4 + b, i] = block

    sums = []

    def stream(r, s):
        first, blocks, order, way = STREAMS[r][s]
        where = {"x": pl.ds(0, 2), "y": pl.ds(0, NY), "z": pl.ds(0, NZ)}
        mine = {"x": xl, "y": y, "z": z}

        def chunk(places):
            at = {**where, **{axis: pl.ds(place, 1) for axis, place in places.items()}}
            return part.at[r, pl.ds(first, blocks), at["x"], at["y"], at["z"]]

        def send(places, key, to):
            i = number[key]
            copy = remote(chunk(places), landing[key], rs_s.at[i], rs_r.at[i], to)
            copy.start()
            sums.append(copy)

        def wait(key):
            i = number[key]
            pltpu.make_async_copy(landing[key], landing[key], rs_r.at[i]).wait()

        def own_sum(keys):
            for key in keys:
                wait(key)
            total = chunk({})[...].astype(F32)
            for key in keys:
                total = total + landing[key][...].astype(F32)
            return total

        pending = []
        for stage in order:
            if pending:
                chunk({})[...] = own_sum(pending).astype(BF16)
            if stage in ("y", "z"):
                n, me = SIZES[stage], mine[stage]
                by = y_by if stage == "y" else z_by
                hops = hops_of(stage, way)
                for d in (1, -1):
                    send({stage: (me + d * hops[d] + n) % n}, (r, s, stage, d, 1), by((d + n) % n))
                yield
                for hop in range(2, n // 2 + 1):
                    for d in (way, -way):
                        if hop > hops[d]:
                            continue
                        to = {stage: (me + d * (hops[d] - hop + 1) + n) % n}
                        came = (r, s, stage, d, hop - 1)
                        wait(came)
                        here = chunk(to)
                        here[...] = (here[...].astype(F32) + landing[came][...].astype(F32)).astype(BF16)
                        send(to, (r, s, stage, d, hop), by((d + n) % n))
                        yield
                pending = [(r, s, stage, d, hops[d]) for d in (1, -1)]
                where[stage] = pl.ds(me, 1)
            else:
                axes = stage.rstrip("d")
                pending = []
                for offset in offsets(stage):
                    to = {axis: (mine[axis] + by) % SIZES[axis] for axis, by in zip(axes, offset)}
                    names = {"x": "xl", "y": "y", "z": "z"}
                    send(to, (r, s, stage, offset), device(**{names[axis]: place for axis, place in to.items()}))
                    pending.append((r, s, stage, offset))
                yield
                for axis in axes:
                    where[axis] = pl.ds(mine[axis], 1)
        total = own_sum(pending).astype(BF16)
        for b in range(blocks):
            gw_ref[r, :, pl.ds((first + b) * 128, 128)] = total[b, 0, 0, 0]

    def decay_sum():
        for i, (buffer, by, n) in enumerate(((dy, y_by, NY), (dz, z_by, NZ), (dx, lambda k: to_xl, 2))):
            copies = []
            for k in range(1, n):
                copies.append(remote(dv, buffer.at[k - 1], dv_s.at[i * 8 + k], dv_r.at[i * 8 + k], by(k)))
                copies[-1].start()
            yield
            for copy in copies:
                copy.wait()
            total = dv[...]
            for k in range(n - 1):
                total = total + buffer[k]
            dv[...] = total
        gd_ref[...] = pltpu.roll(dv[...], (C - dp * 16) % C, axis=1)

    start = 2 - 2 * xh
    local[2].wait()
    local[4].wait()
    for copy in dec_copies:
        copy.wait_recv()

    def forward_loop(low, high):
        def body(layer, carry):
            forward(layer)
            return carry

        lax.fori_loop(low, high, body, 0)

    forward_loop(0, start)
    first_hop(0)
    first_hop(1)
    second_hop(0)
    first_hop(2)
    second_hop(1)
    rest(0)
    first_hop(3)
    second_hop(2)
    rest(1)
    forward(start)
    forward(start + 1)
    second_hop(3)
    rest(2)
    forward(start + 2)
    rest(3)
    forward_loop(start + 3, 8)

    local[3].wait()
    count = 4 - 2 * xh

    def body(i, carry):
        backward(7 - i)
        return carry

    lax.fori_loop(0, count, body, 0)
    weight_gradient(1, 0)
    pieces = [functools.partial(weight_gradient, 1, 1)]
    pieces += [functools.partial(backward, 7 - count - i, i < 3) for i in range(4)]
    pieces += [functools.partial(weight_gradient, 0, n) for n in range(2)]
    streams = {r * 16 + s: stream(r, s) for r in range(2) for s in range(len(STREAMS[r]))}
    streams[-2] = decay_sum()

    def advance(key):
        if key == -1:
            pieces.pop(0)()
        elif next(streams[key], 0) is not None:
            del streams[key]

    for key in ORDER:
        advance(key)
    assert not streams and not pieces

    for copy in sums:
        copy.wait_send()
    for copy in dec_copies:
        copy.wait_send()
    direct = sum(route[i] == "xh" for route in (PLUS, MINUS) for i in range(8))
    sent = w.at[0, pl.ds(0, (8 + direct) * UNIT)]
    pltpu.make_async_copy(sent, sent, xh_s).wait()
    for q in range(4):
        parts = (q, q + 2) if q < 2 else (2 * q, 2 * q + 1)
        passed = sum(5 + (PLUS[p] != "xh") + (MINUS[p] != "xh") for p in parts)
        sent = w.at[0, pl.ds(0, passed * UNIT + 512)]
        pltpu.make_async_copy(sent, sent, gs.at[q]).wait()
    for r in range(2):
        pltpu.make_async_copy(w.at[0], w.at[0], cw_s.at[r]).wait()
        pltpu.make_async_copy(p_act.at[r], p_act.at[r], pa_s.at[r]).wait()
        pltpu.make_async_copy(p_gq.at[r], p_gq.at[r], pg_s.at[r]).wait()
        pltpu.make_async_copy(dd_in.at[r], dd_in.at[r], dd_s.at[r]).wait()


def hand_on(gw_in, gd_in, gw_ref, gd_ref):
    gw_ref[...] = gw_in[...]
    gd_ref[...] = gd_in[:, :16]


def on_device(currents, weights, decay, out_grad):
    dma = pltpu.SemaphoreType.DMA
    vmem = pltpu.VMEM
    scratch = [
        vmem((8, C, C), BF16),
        vmem((9, ROWS, C), BF16),
        vmem((8, 4, HALF, C), F32),
        vmem((8, ROWS, C), BF16),
        vmem((ROWS, C), BF16),
        vmem((2, ROWS, C), BF16),
        vmem((2, ROWS, C), BF16),
        vmem((2, 8, 2, NY, NZ, 16, 128), BF16),
        vmem((4, 2, 1, C), F32),
        vmem((8, 1, C), F32),
        vmem((2, 1, C), F32),
        vmem((2, C), F32),
        vmem((NY - 1, 2, C), F32),
        vmem((NZ - 1, 2, C), F32),
        vmem((1, 2, C), F32),
        dma((5,)), dma((2, 3)), dma((2,)), dma((2,)), dma, dma((4, SUBS, 8)), dma((4,)), dma((4, SUBS)),
        dma((2,)), dma((2,)), dma((2,)), dma((2,)), dma((2,)), dma((2,)), dma((24,)), dma((24,)),
        dma((len(KEYS),)), dma((len(KEYS),)),
    ] + [vmem(PLAN[key], BF16) for key in KEYS]
    anywhere = pl.BlockSpec(memory_space=pl.ANY)
    in_vmem = pl.BlockSpec(memory_space=pltpu.VMEM)
    gw, gd = pl.pallas_call(
        kernel,
        out_shape=(jax.ShapeDtypeStruct((2, 16, C), BF16), jax.ShapeDtypeStruct((2, C), F32)),
        in_specs=[anywhere] * 4,
        out_specs=(in_vmem, in_vmem),
        scratch_shapes=scratch,
        compiler_params=pltpu.CompilerParams(
            collective_id=0, has_side_effects=True, vmem_limit_bytes=60 * 2**20
        ),
        name="relay",
    )(
        currents.reshape(2, ROWS, C),
        weights.reshape(2, C, C),
        decay,
        out_grad.reshape(2, ROWS, C),
    )
    gw, gd = pl.pallas_call(
        hand_on,
        out_shape=(jax.ShapeDtypeStruct((2, 16, C), BF16), jax.ShapeDtypeStruct((2, 16), F32)),
        in_specs=[in_vmem] * 2,
        out_specs=(in_vmem, in_vmem),
        name="results",
    )(gw, gd)
    return gw[:, None], gd[:, None]


def solution(mesh):
    in_specs = (
        P(None, None, "dp", None),
        P(None, "section", None, None),
        P(None, "section", None),
        P(None, None, "dp", None),
    )
    out_specs = (P(None, "section", "dp", None), P(None, "section", "dp"))
    return jax.shard_map(on_device, mesh=mesh, in_specs=in_specs, out_specs=out_specs, check_vma=False)
```
